128 devices in a mesh: nodes: 32 (over y, z, core), tm: 4 (over x).
Axes of the slice: x: 4, y: 4, z: 4, core: 2. Of those that a mesh axis runs over, the one named last changes fastest.
Arguments:
- memory: float32 [32768, 512], P('nodes'), may hold values from -128 to 128
- end_owner: int32 [2, 32768, 1], P(None, ('nodes', 'tm')), may hold values from 0 to 31; in each aligned block of 256 rows (0 to 255, 256 to 511, ..., all dimensions but the last counted through in order) at most 16 rows name the same one
- end_row: int32 [2, 32768], P(None, ('nodes', 'tm')), may hold values from 0 to 1023
- nbr_owner: int32 [2, 327680, 1], P(None, ('nodes', 'tm')), may hold values from 0 to 31; in each aligned block of 2560 rows (0 to 2559, 2560 to 5119, ..., all dimensions but the last counted through in order) at most 160 rows name the same one
- nbr_row: int32 [2, 327680], P(None, ('nodes', 'tm')), may hold values from 0 to 1023
- event_ticks: int32 [2, 16384], P(None, ('nodes', 'tm')), may hold values from 4096 to 8191
- nbr_ticks: int32 [2, 327680], P(None, ('nodes', 'tm')), may hold values from 0 to 4095
- nbr_count: int32 [2, 32768], P(None, ('nodes', 'tm')), may hold values from 1 to 10
- time_freq: float32 [512], replicated, may hold values from 0.0002 to 0.5
- time_phase: float32 [512], replicated, may hold values from -3.140625 to 3.140625
- w_query: bfloat16 [512, 512], replicated, may hold values from -0.25 to 0.25
- w_key_value: bfloat16 [512, 1024], replicated, may hold values from -0.25 to 0.25
- w_out: bfloat16 [512, 512], replicated, may hold values from -0.25 to 0.25
- gru_input: bfloat16 [1024, 1536], replicated, may hold values from -0.1875 to 0.1875
- gru_hidden: bfloat16 [512, 1536], replicated, may hold values from -0.25 to 0.25
- gru_bias: float32 [1536], replicated, may hold values from -3 to 3
Outputs:
- embeddings: float32 [2, 32768, 512], P(None, ('nodes', 'tm'))
- new_memory: float32 [32768, 512], P('nodes')
The draws below stay inside these ranges and needn't reach their ends.
Inputs may be any that keep to these rules, and one draw needn't show every extreme that they name: `end_owner`: among one device's endpoint rows of one batch (aligned blocks of 256 rows), at most 16 name one owner, a bound that some block reaches. `nbr_owner`: among one device's neighbour rows of one batch (aligned blocks of 2560 rows), at most 160 name one owner, a bound that some block reaches.
All inputs are finite; a program needn't handle non-finite values.
Results may differ from the reference program's by a relative error of at most 0.013.
The reference program's roundings to bfloat16 on the way count: a program that leaves them out, or rounds other values in their place, can miss the bound.
Values may be sent and summed in bfloat16 or wider, within the bound.
No kernel may reach another device: no remote copies, remote signals or barrier semaphores. Data moves between devices by JAX's collectives and lax.ppermute only.
A program may use at most 192 MiB of HBM per device.

```python
import math
import jax
import jax.numpy as jnp
import numpy as np
from jax import lax

MEM = 512
HEADS = 4
NBR = 10
BATCHES = 2
EV_DEV = 128
NODE_DEV = 1024
HEAD_DIM = 128
EVENTS = 16384
ENDS = 32768
NBRS = 327680
NODES = 32768
CAP_END = 16
CAP_NBR = 160
N_NODES = 32


def draw_memory(key, part):
    key = jax.random.fold_in(key, 11)
    base_key, column_key, row_key = jax.random.split(key, 3)
    base = jax.random.truncated_normal(base_key, -4.0, 4.0, (NODES, MEM), jnp.float32)
    column_scale = jnp.exp(jax.random.uniform(column_key, (1, MEM), jnp.float32, math.log(0.5), math.log(2.0)))
    row_scale = jnp.exp(jax.random.uniform(row_key, (NODES, 1), jnp.float32, math.log(0.5), math.log(2.0)))
    return base * row_scale * column_scale * 0.5


def set_ends(result, key, least, top_value):
    longest = result.shape.index(max(result.shape))
    spots = []
    for shift in (0, 1):
        where = [jax.random.randint(jax.random.fold_in(key, axis), (), 0, length) for axis, length in enumerate(result.shape)]
        where[longest] = (where[longest] + shift) % result.shape[longest]
        spots.append(tuple(where))
    return result.at[spots[0]].set(least).at[spots[1]].set(top_value)


def cumulative_ranks(count, lean):
    portions = [(1 << 20) // math.isqrt(rank ** lean) + 1 for rank in range(1, count + 1)]
    spread = 1 + sum(portions) // (1 << 30)
    return np.cumsum(np.array([max(1, weight // spread) for weight in portions]))


def ranked(key, shape, amount, lean):
    grid = cumulative_ranks(amount, lean)
    pick = jax.random.randint(jax.random.fold_in(key, 1), shape, 0, int(grid[amount - 1]))
    rank = jnp.searchsorted(jnp.asarray(grid, jnp.int32), pick, side="right")
    return jax.random.permutation(jax.random.fold_in(key, 2), amount)[rank].astype(jnp.int32)


def deal_out(own_key, own, number, rows, number_of, top, limit, slope):
    ranking = jax.random.permutation(own_key, number_of)
    crowded, common = load_shares(number_of, rows * top, limit, slope, True), load_shares(number_of, rows * top, limit, slope, False)
    places = jnp.arange(number_of)

    def named(tallies, offset_by):
        used = int((tallies > 0).sum())
        fixed = max(1, used // 4)
        shifted = fixed + (places - fixed + offset_by * (used - fixed)) % max(1, number_of - fixed)
        return jnp.zeros((number_of,), jnp.int32).at[ranking[jnp.where(places < fixed, places, shifted)]].set(jnp.asarray(tallies, jnp.int32))

    tallies = jnp.where(number % 4 == 0, named(crowded, number // 4), named(common, number - number // 4 - 1))
    mixed = jax.random.permutation(jax.random.fold_in(own, 3), number_of)
    giver, taker = mixed[0:number_of // 2 * 2:2], mixed[1:number_of // 2 * 2:2]
    slack = jnp.minimum(tallies[giver] - 1, limit - tallies[taker]) // 2
    slack = jnp.where((giver == ranking[0]) | (taker == ranking[0]) | (tallies[taker] == 0), 0, jnp.maximum(slack, 0))
    shifted = jax.random.randint(jax.random.fold_in(own, 4), (number_of // 2,), 0, 1 << 20) % (slack + 1)
    tallies = tallies.at[giver].add(-shifted).at[taker].add(shifted)
    items = jnp.searchsorted(jnp.cumsum(tallies), jnp.arange(rows * top), side="right").astype(jnp.int32)
    listing = items.reshape(top, rows).T
    listing = listing[jax.random.permutation(jax.random.fold_in(own, 1), rows)]
    offset_by = jax.random.randint(jax.random.fold_in(own, 2), (rows, 1), 0, top)
    return jnp.take_along_axis(listing, (jnp.arange(top)[None, :] + offset_by) % top, axis=1)


def load_shares(number_of, total, limit, skew, full):
    portions = [(1 << 20) // math.isqrt(grade ** skew) + 1 for grade in range(1, number_of + 1)]
    largest = limit if full else min(limit, max(-(-total // number_of), total * portions[0] // sum(portions)))
    least = 1 if total - largest >= number_of - 1 else 0
    counts, spare = [largest] + [least] * (number_of - 1), total - largest - least * (number_of - 1)
    while spare > 0:
        movable = [i for i in range(1, number_of) if counts[i] < largest] or [i for i in range(1, number_of) if counts[i] < limit]
        pool, budget = sum([portions[i] for i in movable]), spare
        for i in movable:
            extra = min(limit - counts[i], max(1, budget * portions[i] // pool), spare)
            counts[i] = counts[i] + extra
            spare = spare - extra
    return np.array(counts)


def centred(key, shape, scale, limit, kind=jnp.bfloat16):
    return jnp.clip(scale * jax.random.normal(key, shape, jnp.float32), -limit, limit).astype(kind)


def setup_inputs(seed: int = 0) -> dict:
    key_list = jax.random.split(jax.random.key(seed), 17)
    memory = draw_memory(jax.random.fold_in(key_list[16], 71), 0)
    end_owner_keys = jax.random.split(jax.random.fold_in(key_list[1], 1), BATCHES * ENDS // (2 * EV_DEV))
    end_owner_turns = jax.random.permutation(jax.random.fold_in(key_list[1], 3), BATCHES * ENDS // (2 * EV_DEV))
    end_owner = jax.vmap(lambda own, number: deal_out(jax.random.fold_in(key_list[1], 2), own, number, 2 * EV_DEV, N_NODES, 1, CAP_END, 2))(end_owner_keys, end_owner_turns).reshape((BATCHES, ENDS, 1))
    end_row = set_ends(ranked(key_list[2], (BATCHES, ENDS), NODE_DEV, 2), jax.random.fold_in(key_list[2], 3), 0, NODE_DEV - 1).astype(jnp.int32)
    nbr_owner_keys = jax.random.split(jax.random.fold_in(key_list[3], 1), BATCHES * NBRS // (20 * EV_DEV))
    nbr_owner_turns = jax.random.permutation(jax.random.fold_in(key_list[3], 3), BATCHES * NBRS // (20 * EV_DEV))
    nbr_owner = jax.vmap(lambda own, number: deal_out(jax.random.fold_in(key_list[3], 2), own, number, 20 * EV_DEV, N_NODES, 1, CAP_NBR, 2))(nbr_owner_keys, nbr_owner_turns).reshape((BATCHES, NBRS, 1))
    nbr_row = set_ends(ranked(key_list[4], (BATCHES, NBRS), NODE_DEV, 2), jax.random.fold_in(key_list[4], 3), 0, NODE_DEV - 1).astype(jnp.int32)
    event_ticks = set_ends(jax.random.randint(key_list[5], (BATCHES, EVENTS), 4096, 8192), jax.random.fold_in(key_list[5], 1), 4096, 8191).astype(jnp.int32)
    nbr_ticks = set_ends(jax.random.randint(key_list[6], (BATCHES, NBRS), 0, 4096), jax.random.fold_in(key_list[6], 1), 0, 4095).astype(jnp.int32)
    nbr_count = set_ends(jax.random.randint(key_list[7], (BATCHES, ENDS), 1, NBR + 1), jax.random.fold_in(key_list[7], 1), 1, NBR).astype(jnp.int32)
    time_freq = jnp.clip(jnp.exp(jax.random.uniform(key_list[8], (MEM,), jnp.float32, math.log(0.0002), math.log(0.5))), 0.0002, 0.5)
    time_phase = jnp.clip(jax.random.uniform(key_list[9], (MEM,), jnp.float32, -3.140625, 3.140625), -3.140625, 3.140625)
    w_query = centred(key_list[10], (MEM, MEM), MEM ** -0.5, 0.25)
    w_key_value = centred(key_list[11], (MEM, 2 * MEM), MEM ** -0.5, 0.25)
    w_out = centred(key_list[12], (MEM, MEM), MEM ** -0.5, 0.25)
    gru_input = centred(key_list[13], (2 * MEM, 3 * MEM), (2 * MEM) ** -0.5, 0.1875)
    gru_hidden = centred(key_list[14], (MEM, 3 * MEM), MEM ** -0.5, 0.25)
    gru_bias = centred(key_list[15], (3 * MEM,), 0.5, 3.0, jnp.float32)
    return {"memory": memory, "end_owner": end_owner, "end_row": end_row, "nbr_owner": nbr_owner, "nbr_row": nbr_row, "event_ticks": event_ticks, "nbr_ticks": nbr_ticks, "nbr_count": nbr_count, "time_freq": time_freq, "time_phase": time_phase, "w_query": w_query, "w_key_value": w_key_value, "w_out": w_out, "gru_input": gru_input, "gru_hidden": gru_hidden, "gru_bias": gru_bias}


def attend(self_rows, nbr_rows, tick_gaps, nbr_valid, time_freq, time_phase, w_query, w_key_value, w_out):
    row_total = self_rows.shape[0]
    encoding = jnp.cos(tick_gaps[:, None] * time_freq[None, :] + time_phase[None, :])
    key_in = (nbr_rows.astype(jnp.float32) + encoding).astype(jnp.bfloat16)
    queries = jnp.dot(self_rows, w_query, preferred_element_type=jnp.float32).astype(jnp.bfloat16)
    queries = queries.reshape(row_total, HEADS, HEAD_DIM)
    packed = jnp.dot(key_in, w_key_value, preferred_element_type=jnp.float32).astype(jnp.bfloat16)
    packed = packed.reshape(row_total, NBR, 2, HEADS, HEAD_DIM)
    scores = jnp.einsum('ehd,ekhd->ehk', queries.astype(jnp.float32), packed[:, :, 0].astype(jnp.float32)) / math.sqrt(HEAD_DIM)
    valid_mask = jnp.arange(NBR, dtype=jnp.int32)[None, None, :] < nbr_valid[:, None, None]
    scores = jnp.where(valid_mask, scores, -1e+30)
    top_score = lax.optimization_barrier(jnp.max(scores, axis=2, keepdims=True))
    raised = jnp.exp(scores - top_score)
    weights = (raised / lax.optimization_barrier(jnp.sum(raised, axis=2, keepdims=True))).astype(jnp.bfloat16)
    attended = jnp.einsum('ehk,ekhd->ehd', weights.astype(jnp.float32), packed[:, :, 1].astype(jnp.float32))
    attended = attended.reshape(row_total, HEADS * HEAD_DIM).astype(jnp.bfloat16)
    return self_rows.astype(jnp.float32) + jnp.dot(attended, w_out, preferred_element_type=jnp.float32)

def gru_update(memory_now, node_sums, node_counts, gru_input, gru_hidden, gru_bias):
    pulled = memory_now.astype(jnp.bfloat16)
    mean_message = (node_sums / jnp.maximum(node_counts, 1.0)[:, None]).astype(jnp.bfloat16)
    gru_in = jnp.concatenate([pulled, mean_message], axis=1)
    gates_in = jnp.dot(gru_in, gru_input, preferred_element_type=jnp.float32) + gru_bias[None, :]
    gates_hid = jnp.dot(pulled, gru_hidden, preferred_element_type=jnp.float32)
    reset_gate = jax.nn.sigmoid(gates_in[:, :MEM] + gates_hid[:, :MEM])
    update_gate = jax.nn.sigmoid(gates_in[:, MEM:2 * MEM] + gates_hid[:, MEM:2 * MEM])
    candidate = jnp.tanh(gates_in[:, 2 * MEM:] + reset_gate * gates_hid[:, 2 * MEM:])
    updated = (1.0 - update_gate) * candidate + update_gate * memory_now
    return jnp.where(node_counts[:, None] > 0, updated, memory_now)

def reference(memory, end_owner, end_row, nbr_owner, nbr_row, event_ticks, nbr_ticks, nbr_count, time_freq, time_phase, w_query, w_key_value, w_out, gru_input, gru_hidden, gru_bias):
    memory_now = memory
    outputs = []
    block_rows = 2 * EV_DEV
    block_total = ENDS // block_rows
    for batch in range(BATCHES):
        pulled = memory_now.astype(jnp.bfloat16)
        end_node = end_owner[batch, :, 0] * NODE_DEV + end_row[batch]
        nbr_node = nbr_owner[batch, :, 0] * NODE_DEV + nbr_row[batch]
        tick_gaps = (jnp.repeat(event_ticks[batch], 2 * NBR) - nbr_ticks[batch]).astype(jnp.float32)

        def one_block(pieces):
            end_ids, nbr_ids, block_gaps, block_valid = pieces
            return attend(pulled[end_ids], pulled[nbr_ids], block_gaps, block_valid, time_freq, time_phase, w_query, w_key_value, w_out)
        embedded = lax.map(one_block, (end_node.reshape(block_total, block_rows), nbr_node.reshape(block_total, block_rows * NBR), tick_gaps.reshape(block_total, block_rows * NBR), nbr_count[batch].reshape(block_total, block_rows)))
        outputs.append(embedded.reshape(ENDS, MEM))
        self_rows = pulled[end_node]
        partner = self_rows.reshape(EVENTS, 2, MEM)[:, ::-1].reshape(ENDS, MEM)
        node_sums = jax.ops.segment_sum(partner.astype(jnp.float32), end_node, NODES)
        node_counts = jax.ops.segment_sum(jnp.ones((ENDS,), jnp.float32), end_node, NODES)
        memory_now = gru_update(memory_now, node_sums, node_counts, gru_input, gru_hidden, gru_bias)
    return (jnp.stack(outputs), memory_now)
```

```python
import functools
import math

import jax
import jax.numpy as jnp
import numpy as np
from jax import lax
from jax.experimental import pallas as pl
from jax.experimental.pallas import tpu as pltpu
from jax.sharding import PartitionSpec as P

HEADS = 4
NBR = 10
HEAD_DIM = 128
CAP_END = 16
CAP_NBR = 160
SLOTS = 256
GROUP = 8
F32 = jnp.float32
BF16 = jnp.bfloat16
VMEM_LIMIT = 56 * 1024 * 1024
NONE = -1e30
NT = (((1,), (1,)), ((), ()))
COS_TERMS = tuple(
    np.polynomial.chebyshev.Chebyshev.interpolate(
        lambda u: np.cos(2 * np.pi * np.sqrt(u)), 7, domain=[0.0, 0.25]
    )
    .convert(kind=np.polynomial.Polynomial)
    .coef.tolist()
)


def params(steps=None):
    return pltpu.CompilerParams(vmem_limit_bytes=VMEM_LIMIT)


def cost(flops, size):
    return pl.CostEstimate(flops=int(flops), bytes_accessed=int(size), transcendentals=0)


def iota(shape, dim):
    return lax.broadcasted_iota(jnp.int32, shape, dim)


def place_kernel(
    node_dev,
    end_owner_ref,
    end_row_ref,
    nbr_owner_ref,
    nbr_row_ref,
    event_ticks_ref,
    nbr_ticks_ref,
    nbr_count_ref,
    ids_ref,
    ends_ref,
    gap_ref,
    slot_ref,
):
    batches, ends = end_row_ref.shape
    nbrs = nbr_row_ref.shape[1]
    peers = ids_ref.shape[0]
    block = ends
    upper = (iota((block, block), 0) < iota((block, block), 1)).astype(BF16)
    lane_e = iota((ends // 2, nbrs), 1) - 2 * NBR * iota((ends // 2, nbrs), 0)
    spread_event = ((lane_e >= 0) & (lane_e < 2 * NBR)).astype(BF16)
    lane_n = iota((ends, nbrs), 1) - NBR * iota((ends, nbrs), 0)
    inside = (lane_n >= 0) & (lane_n < NBR)
    spread_end = inside.astype(BF16)
    place_in_end = jnp.sum(jnp.where(inside, lane_n, 0), axis=0, keepdims=True).astype(F32)
    end_index = jnp.sum(jnp.where(inside, iota((ends, nbrs), 0), 0), axis=0, keepdims=True).astype(F32)
    row8 = iota((8, 1), 0)
    peer_col = iota((peers, 1), 0)
    for b in range(batches):
        ticks = event_ticks_ref[b : b + 1, :]
        halves = jnp.where(row8 == 0, ticks >> 7, ticks & 127).astype(F32).astype(BF16)
        spread = jnp.dot(halves, spread_event, preferred_element_type=F32)
        gap = spread[0:1] * 128.0 + spread[1:2] - nbr_ticks_ref[b : b + 1, :].astype(F32)
        counts = jnp.broadcast_to(nbr_count_ref[b : b + 1, :].astype(F32), (8, ends)).astype(BF16)
        count = jnp.dot(counts, spread_end, preferred_element_type=F32)[0:1]
        valid = place_in_end < count
        nbr_owner = jnp.where(valid, nbr_owner_ref[b : b + 1, :], -1)
        owned_nbr = jnp.where(nbr_owner == peer_col, 1.0, 0.0)
        owned_end = jnp.where(end_owner_ref[b : b + 1, :] == peer_col, 1.0, 0.0)
        offset = jnp.zeros((peers, 1), F32)
        ranks = []
        for j in range(nbrs // block):
            part = owned_nbr[:, j * block : (j + 1) * block]
            before = jnp.dot(part.astype(BF16), upper, preferred_element_type=F32)
            ranks.append(jnp.sum(part * (before + offset), axis=0, keepdims=True))
            offset = offset + jnp.sum(part, axis=1, keepdims=True)
        before = jnp.dot(owned_end.astype(BF16), upper, preferred_element_type=F32)
        end_rank = jnp.sum(owned_end * before, axis=0, keepdims=True)
        end_owner = end_owner_ref[b : b + 1, :].astype(F32)
        slot_ref[b : b + 1, :] = (end_owner * CAP_END + end_rank).astype(jnp.int32)
        nbr_rank = jnp.where(valid, jnp.concatenate(ranks, axis=1), -1.0)
        rank = jnp.concatenate([nbr_rank, end_rank + CAP_NBR], axis=1)
        at_slot = jnp.where(iota((SLOTS, 1), 0).astype(F32) == rank, 1.0, 0.0).astype(BF16)
        owned = jnp.concatenate([owned_nbr, owned_end], axis=1)
        row = jnp.concatenate([nbr_row_ref[b : b + 1, :], end_row_ref[b : b + 1, :]], axis=1)
        none = jnp.zeros((1, ends), F32)
        gap_int = jnp.concatenate([gap, none], axis=1).astype(jnp.int32)
        whose = jnp.concatenate([end_index, none], axis=1)
        named = [
            (row >> 5).astype(F32),
            (row & 31).astype(F32),
            jnp.ones(row.shape, F32),
            whose,
        ]
        named = jnp.concatenate([(owned * v).astype(BF16) for v in named], axis=0)
        lists = lax.dot_general(named, at_slot, NT, preferred_element_type=F32)
        wanted, high = lists[2 * peers : 3 * peers] > 0.5, lists[0:peers]
        ids = high * 32.0 + lists[peers : 2 * peers]
        ids_ref[:, b * SLOTS : (b + 1) * SLOTS] = jnp.where(wanted, ids, float(node_dev)).astype(jnp.int32)
        ends_ref[b] = jnp.where(wanted, lists[3 * peers : 4 * peers], -1.0).astype(jnp.int32)
        timed = [(gap_int >> 7).astype(F32), (gap_int & 127).astype(F32)]
        timed = jnp.concatenate([(owned * v).astype(BF16) for v in timed], axis=0)
        gaps = lax.dot_general(at_slot, timed, NT, preferred_element_type=F32)
        gap_ref[b] = gaps[:, 0:peers] * 128.0 + gaps[:, peers : 2 * peers]


def place(node_dev, peers, end_owner, end_row, nbr_owner, nbr_row, event_ticks, nbr_ticks, nbr_count):
    batches, ends = end_row.shape
    return pl.pallas_call(
        functools.partial(place_kernel, node_dev),
        out_shape=(
            jax.ShapeDtypeStruct((peers, batches * SLOTS), jnp.int32),
            jax.ShapeDtypeStruct((batches, peers, SLOTS), jnp.int32),
            jax.ShapeDtypeStruct((batches, SLOTS, peers), F32),
            jax.ShapeDtypeStruct((batches, ends), jnp.int32),
        ),
        compiler_params=params(),
        cost_estimate=cost(2e9, 1e6),
        name="request_lists",
    )(end_owner, end_row, nbr_owner, nbr_row, event_ticks, nbr_ticks, nbr_count)


def lookup_kernel(ranges, ids_ref, rows_ref, found_ref):
    node_dev = rows_ref.shape[0]
    ids = jnp.concatenate([ids_ref[0, lo:hi, :] for lo, hi in ranges], axis=0)
    lane = iota((1, node_dev), 1)
    picks = [(ids[:, p : p + 1] == lane).astype(F32).astype(BF16) for p in range(GROUP)]
    picked = jnp.dot(jnp.concatenate(picks, axis=0), rows_ref[...], preferred_element_type=F32)
    found_ref[...] = picked.astype(BF16).reshape(found_ref.shape)


def lookup(ranges, asked, pulled):
    groups, listed, _ = asked.shape
    cap = sum(hi - lo for lo, hi in ranges)
    node_dev, width = pulled.shape
    peers = groups * GROUP
    return pl.pallas_call(
        functools.partial(lookup_kernel, ranges),
        grid=(groups,),
        in_specs=[
            pl.BlockSpec((1, listed, GROUP), lambda g: (g, 0, 0)),
            pl.BlockSpec((node_dev, width), lambda g: (0, 0)),
        ],
        out_specs=pl.BlockSpec((GROUP, cap, width), lambda g: (g, 0, 0)),
        out_shape=jax.ShapeDtypeStruct((peers, cap, width), BF16),
        compiler_params=params(),
        cost_estimate=cost(2 * peers * cap * node_dev * width, 2 * peers * cap * width),
        name="lookup_rows",
    )(asked, pulled)


def ends_kernel(slot_ref, slot_col_ref, pair_col_ref, found_ref, self_ref, push_ref):
    slots = push_ref.shape[0] * push_ref.shape[1]
    width = found_ref.shape[2]
    found = found_ref[...].reshape(slots, width)
    lane = iota((1, slots), 1)
    own = (slot_col_ref[...] == lane).astype(F32).astype(BF16)
    self_ref[...] = jnp.dot(own, found, preferred_element_type=F32).astype(BF16)
    pair = (pair_col_ref[...] == lane).astype(F32).astype(BF16)
    partner = jnp.dot(pair, found, preferred_element_type=F32).astype(BF16)
    to_slot = (iota((slots, 1), 0) == slot_ref[...]).astype(F32).astype(BF16)
    push = jnp.dot(to_slot, partner, preferred_element_type=F32).astype(BF16)
    push_ref[...] = push.reshape(push_ref.shape)


def end_rows(slot, found):
    ends = slot.shape[0]
    peers, _, width = found.shape
    pair = slot.reshape(-1, 2)[:, ::-1].reshape(-1)
    whole = lambda *shape: pl.BlockSpec(shape, lambda g: (0,) * len(shape))
    return pl.pallas_call(
        ends_kernel,
        grid=(1,),
        in_specs=[
            whole(1, ends),
            whole(ends, 1),
            whole(ends, 1),
            whole(peers, CAP_END, width),
        ],
        out_specs=(whole(ends, width), whole(peers, CAP_END, width)),
        out_shape=(
            jax.ShapeDtypeStruct((ends, width), BF16),
            jax.ShapeDtypeStruct((peers, CAP_END, width), BF16),
        ),
        compiler_params=params(),
        cost_estimate=cost(1e9, 2e6),
        name="end_rows",
    )(slot[None, :], slot[:, None], pair[:, None], found)


def cos_turns(turns):
    part = turns - jnp.floor(turns + 0.5)
    square = part * part
    value = COS_TERMS[-1] * square + COS_TERMS[-2]
    for term in COS_TERMS[-3::-1]:
        value = value * square + term
    return value


def attend_kernel(
    ranges,
    skip,
    first,
    last,
    found_ref,
    gap_ref,
    ends_ref,
    self_ref,
    turn_ref,
    w_query_ref,
    w_key_value_ref,
    w_out_ref,
    *refs,
):
    refs = list(refs)
    if not first:
        top_in, total_in, acc_in = refs[:3]
        refs = refs[3:]
    if last:
        out_ref, query_ref, top_ref, total_ref, acc_ref = refs
    else:
        top_ref, total_ref, acc_ref, query_ref = refs
    step = pl.program_id(0)
    ends, width = self_ref.shape

    @pl.when(step == 0)
    def _():
        query = jnp.dot(self_ref[...], w_query_ref[...], preferred_element_type=F32)
        query_ref[...] = query.astype(BF16)
        if first:
            top_ref[...] = jnp.full(top_ref.shape, NONE, F32)
            total_ref[...] = jnp.zeros(total_ref.shape, F32)
            acc_ref[...] = jnp.zeros(acc_ref.shape, F32)
        else:
            top_ref[...] = top_in[...]
            total_ref[...] = total_in[...]
            acc_ref[...] = acc_in[...]

    freq, phase = turn_ref[0:1, :], turn_ref[1:2, :]
    keyed = []
    for p in range(GROUP):
        gap = jnp.concatenate([gap_ref[0, lo:hi, p : p + 1] for lo, hi in ranges], axis=0)
        row = found_ref[p, skip:, :].astype(F32)
        keyed.append((row + cos_turns(gap * freq + phase)).astype(BF16))
    keyed = jnp.concatenate(keyed, axis=0)
    packed = jnp.dot(keyed, w_key_value_ref[...], preferred_element_type=F32).astype(BF16)
    mine = ends_ref[...] == iota((ends, 1), 0)
    scale = 1.0 / math.sqrt(HEAD_DIM)
    for h in range(HEADS):
        lanes = slice(h * HEAD_DIM, (h + 1) * HEAD_DIM)
        score = lax.dot_general(query_ref[:, lanes], packed[:, lanes], NT, preferred_element_type=F32)
        score = jnp.where(mine, score * scale, 2 * NONE)
        top_old = top_ref[:, h : h + 1]
        top = jnp.maximum(top_old, jnp.max(score, axis=1, keepdims=True))
        fade = jnp.exp(top_old - top)
        raised = jnp.exp(score - top)
        top_ref[:, h : h + 1] = top
        total_ref[:, h : h + 1] = total_ref[:, h : h + 1] * fade + jnp.sum(raised, axis=1, keepdims=True)
        value = packed[:, width + h * HEAD_DIM : width + (h + 1) * HEAD_DIM]
        acc_ref[:, lanes] = acc_ref[:, lanes] * fade + jnp.dot(
            raised.astype(BF16), value, preferred_element_type=F32
        )

    if last:

        @pl.when(step == pl.num_programs(0) - 1)
        def _():
            parts = [
                acc_ref[:, h * HEAD_DIM : (h + 1) * HEAD_DIM] / total_ref[:, h : h + 1]
                for h in range(HEADS)
            ]
            attended = jnp.concatenate(parts, axis=1).astype(BF16)
            out_ref[...] = self_ref[...].astype(F32) + jnp.dot(
                attended, w_out_ref[...], preferred_element_type=F32
            )


def attend(ranges, skip, found, gap, whose, self_rows, turn, w_query, w_key_value, w_out, state, last):
    ends, width = self_rows.shape
    peers, held, _ = found.shape
    cap = held - skip
    groups, listed, _ = gap.shape
    whole = lambda *shape: pl.BlockSpec(shape, lambda g: (0,) * len(shape))
    state_shapes = [(ends, HEAD_DIM), (ends, HEAD_DIM), (ends, width)]
    state_specs = [whole(*s) for s in state_shapes]
    state_scratch = [pltpu.VMEM(s, F32) for s in state_shapes]
    query_scratch = [pltpu.VMEM((ends, width), BF16)]
    if last:
        out_specs, out_shape = whole(ends, width), jax.ShapeDtypeStruct((ends, width), F32)
        scratch = query_scratch + state_scratch
    else:
        out_specs = tuple(state_specs)
        out_shape = tuple(jax.ShapeDtypeStruct(s, F32) for s in state_shapes)
        scratch = query_scratch
    return pl.pallas_call(
        functools.partial(attend_kernel, ranges, skip, state is None, last),
        grid=(groups,),
        in_specs=[
            pl.BlockSpec((GROUP, held, width), lambda g: (g, 0, 0)),
            pl.BlockSpec((1, listed, GROUP), lambda g: (g, 0, 0)),
            pl.BlockSpec((1, GROUP * cap), lambda g: (0, g)),
            whole(ends, width),
            whole(8, width),
            whole(width, width),
            whole(width, 2 * width),
            whole(width, width),
        ]
        + ([] if state is None else state_specs),
        out_specs=out_specs,
        out_shape=out_shape,
        scratch_shapes=scratch,
        compiler_params=params(),
        cost_estimate=cost(8 * peers * cap * width * 2 * width, 2 * peers * cap * width),
        name="attend",
    )(found, gap, whose, self_rows, turn, w_query, w_key_value, w_out, *(state or ()))


def gru_kernel(
    order_ref,
    memory_ref,
    ids_ref,
    rows0_ref,
    rows1_ref,
    rows2_ref,
    rows3_ref,
    w_input_ref,
    w_hidden_ref,
    bias_ref,
    *refs,
):
    out_ref, rows_ref, sems = refs[0], refs[-2], refs[-1]
    block, width = memory_ref.shape
    slots = rows0_ref.shape[0]
    step = pl.program_id(0)

    @pl.when(step == 0)
    def _():
        copies = []
        for k, source in enumerate((rows0_ref, rows1_ref, rows2_ref, rows3_ref)):
            at = pl.multiple_of(order_ref[k] * slots, slots)
            copies.append(pltpu.make_async_copy(source, rows_ref.at[pl.ds(at, slots)], sems.at[k]))
        for copy in copies:
            copy.start()
        for copy in copies:
            copy.wait()

    picks = jnp.where(ids_ref[...] == iota((block, 1), 0) + step * block, 1.0, 0.0)
    counts = jnp.sum(picks, axis=1, keepdims=True)
    sums = jnp.dot(picks.astype(BF16), rows_ref[...], preferred_element_type=F32)
    mean = (sums / jnp.maximum(counts, 1.0)).astype(BF16)
    memory = memory_ref[...]
    pulled = memory.astype(BF16)
    dot = functools.partial(jnp.dot, preferred_element_type=F32)
    bias = bias_ref[...]

    def gate(lo, hi):
        own = dot(pulled, w_input_ref[:width, lo:hi]) + dot(mean, w_input_ref[width:, lo:hi])
        return own + bias[:, lo:hi], dot(pulled, w_hidden_ref[:, lo:hi])

    a, c = gate(0, width)
    reset = jax.nn.sigmoid(a + c)
    a, c = gate(2 * width, 3 * width)
    candidate = jnp.tanh(a + reset * c)
    a, c = gate(width, 2 * width)
    update = jax.nn.sigmoid(a + c)
    new = jnp.where(counts > 0, (1.0 - update) * candidate + update * memory, memory)
    out_ref[...] = new
    if len(refs) == 4:
        refs[1][...] = new.astype(BF16)


def gru(order, memory, ids, rows, w_input, w_hidden, bias, with_pulled):
    node_dev, width = memory.shape
    slots = rows[0].shape[0]
    block = 256
    whole = lambda *shape: pl.BlockSpec(shape, lambda g: (0,) * len(shape))
    anywhere = pl.BlockSpec(memory_space=pl.ANY)
    blocked = pl.BlockSpec((block, width), lambda g: (g, 0))
    types = (F32, BF16) if with_pulled else (F32,)
    return pl.pallas_call(
        gru_kernel,
        grid=(node_dev // block,),
        in_specs=[pl.BlockSpec(memory_space=pltpu.SMEM), blocked, whole(1, 4 * slots)]
        + [anywhere] * 4
        + [whole(2 * width, 3 * width), whole(width, 3 * width), whole(1, 3 * width)],
        out_specs=tuple(blocked for _ in types),
        out_shape=tuple(jax.ShapeDtypeStruct((node_dev, width), t) for t in types),
        scratch_shapes=[pltpu.VMEM((4 * slots, width), BF16), pltpu.SemaphoreType.DMA((4,))],
        compiler_params=params(),
        cost_estimate=cost(8e9, 1e7),
        name="memory_update",
    )(order, memory, ids, *rows, w_input, w_hidden, bias)


def exchange(rows):
    return lax.all_to_all(rows, "nodes", split_axis=0, concat_axis=0, tiled=True)


def after(value, earlier):
    return lax.optimization_barrier((value, earlier))[0]


def across_time(value):
    size = lax.axis_size("tm")
    return [value] + [
        lax.ppermute(value, "tm", [(i, (i + k) % size) for i in range(size)]) for k in range(1, size)
    ]


def shards(
    memory,
    end_owner,
    end_row,
    nbr_owner,
    nbr_row,
    event_ticks,
    nbr_ticks,
    nbr_count,
    time_freq,
    time_phase,
    w_query,
    w_key_value,
    w_out,
    gru_input,
    gru_hidden,
    gru_bias,
):
    peers = lax.axis_size("nodes")
    node_dev, width = memory.shape
    batches = end_row.shape[0]
    groups = peers // GROUP
    ids, whose, gaps, end_slot = place(
        node_dev, peers, end_owner[:, :, 0], end_row, nbr_owner[:, :, 0], nbr_row, event_ticks, nbr_ticks, nbr_count
    )
    asked = exchange(ids)
    asked_cols = asked.reshape(groups, GROUP, batches, SLOTS).transpose(2, 0, 3, 1)
    gap_cols = gaps.reshape(batches, SLOTS, groups, GROUP).transpose(0, 2, 1, 3)
    arrived_ids = asked.reshape(peers, batches, SLOTS)[:, :, CAP_NBR : CAP_NBR + CAP_END]
    arrived_ids = arrived_ids.transpose(1, 0, 2).reshape(batches, peers * CAP_END)
    here = lax.axis_index("tm")
    order = jnp.mod(here - jnp.arange(4, dtype=jnp.int32), 4)
    all_ids = jnp.stack(across_time(arrived_ids))[order]
    all_ids = all_ids.transpose(1, 0, 2).reshape(batches, 1, 4 * peers * CAP_END)
    turn = jnp.stack([time_freq, time_phase]) * (1.0 / (2.0 * math.pi))
    turn = jnp.concatenate([turn, jnp.zeros((6, width), F32)])
    bias = gru_bias[None, :]

    end_range = (CAP_NBR, CAP_NBR + CAP_END)
    plans = (
        (((0, CAP_NBR),),),
        (((0, 96),), ((96, CAP_NBR),)),
    )
    pulled = memory.astype(BF16)
    outputs = []
    for b in range(batches):
        found = exchange(lookup((end_range,), asked_cols[b], pulled))
        self_rows, push = end_rows(end_slot[b], found)
        arrived = exchange(push)
        rows = across_time(arrived.reshape(peers * CAP_END, width))
        earlier = arrived
        state = None
        for n, ranges in enumerate(plans[b]):
            last = n == len(plans[b]) - 1
            found = lookup(ranges, asked_cols[b], pulled)
            found = exchange(after(found, earlier))
            earlier = found
            marks = jnp.concatenate([whose[b, :, lo:hi] for lo, hi in ranges], axis=1).reshape(1, -1)
            state = attend(
                ranges, 0, found, gap_cols[b], marks, self_rows, turn, w_query, w_key_value, w_out, state, last
            )
        outputs.append(state)
        updated = gru(order, memory, all_ids[b], rows, gru_input, gru_hidden, bias, b < batches - 1)
        memory = updated[0]
        if b < batches - 1:
            pulled = updated[1]
    return (jnp.stack(outputs), memory)


def solution(mesh):
    return jax.shard_map(
        shards,
        mesh=mesh,
        in_specs=(
            P("nodes", None),
            P(None, ("nodes", "tm"), None),
            P(None, ("nodes", "tm")),
            P(None, ("nodes", "tm"), None),
            P(None, ("nodes", "tm")),
            P(None, ("nodes", "tm")),
            P(None, ("nodes", "tm")),
            P(None, ("nodes", "tm")),
            P(),
            P(),
            P(),
            P(),
            P(),
            P(),
            P(),
            P(),
        ),
        out_specs=(P(None, ("nodes", "tm"), None), P("nodes", None)),
        check_vma=False,
    )
```

```python
import functools
import math

import jax
import jax.numpy as jnp
import numpy as np
from jax import lax
from jax.experimental import pallas as pl
from jax.experimental.pallas import tpu as pltpu
from jax.sharding import PartitionSpec as P

HEADS = 4
NBR = 10
HEAD_DIM = 128
CAP_END = 16
CAP_NBR = 160
SLOTS = 256
CAP_FAST = 80
CAP_EARLY = 48
NBR_BLOCK = 640
F32 = jnp.float32
BF16 = jnp.bfloat16
VMEM_LIMIT = 56 * 1024 * 1024
NT = (((1,), (1,)), ((), ()))
COS_TERMS = tuple(
    np.polynomial.chebyshev.Chebyshev.interpolate(
        lambda u: np.cos(2 * np.pi * np.sqrt(u)), 7, domain=[0.0, 0.25]
    )
    .convert(kind=np.polynomial.Polynomial)
    .coef.tolist()
)


def params(steps=None):
    return pltpu.CompilerParams(vmem_limit_bytes=VMEM_LIMIT)


def cost(flops, size):
    return pl.CostEstimate(flops=int(flops), bytes_accessed=int(size), transcendentals=0)


def iota(shape, dim):
    return lax.broadcasted_iota(jnp.int32, shape, dim)


def before_each(owned, upper, offset):
    size = upper.shape[0]
    counts = []
    for j in range(owned.shape[1] // size):
        part = owned[:, j * size : (j + 1) * size]
        counts.append(jnp.dot(part.astype(BF16), upper, preferred_element_type=F32) + offset)
        offset = offset + jnp.sum(part, axis=1, keepdims=True)
    return jnp.concatenate(counts, axis=1), offset


def place_kernel(
    node_dev,
    end_owner_ref,
    end_row_ref,
    nbr_owner_ref,
    nbr_row_ref,
    event_ticks_ref,
    nbr_ticks_ref,
    nbr_count_ref,
    ids_ref,
    rank_ref,
    gap_ref,
    slot_ref,
):
    batches, ends = end_row_ref.shape
    nbrs = nbr_row_ref.shape[1]
    peers = ids_ref.shape[0]
    upper = (iota((ends, ends), 0) < iota((ends, ends), 1)).astype(F32).astype(BF16)
    lane_e = iota((ends // 2, nbrs), 1) - 2 * NBR * iota((ends // 2, nbrs), 0)
    spread_event = jnp.where((lane_e >= 0) & (lane_e < 2 * NBR), 1.0, 0.0).astype(BF16)
    lane_n = iota((ends, nbrs), 1) - NBR * iota((ends, nbrs), 0)
    inside = (lane_n >= 0) & (lane_n < NBR)
    spread_end = jnp.where(inside, 1.0, 0.0).astype(BF16)
    place_in_end = jnp.sum(jnp.where(inside, lane_n, 0), axis=0, keepdims=True).astype(F32)
    row8 = iota((8, 1), 0)
    peer_col = iota((peers, 1), 0)
    zero = jnp.zeros((peers, 1), F32)
    load = zero
    for b in range(batches):
        ticks = event_ticks_ref[b : b + 1, :]
        halves = jnp.where(row8 == 0, ticks >> 7, ticks & 127).astype(F32).astype(BF16)
        spread = jnp.dot(halves, spread_event, preferred_element_type=F32)
        gap_ref[b : b + 1, :] = spread[0:1] * 128.0 + spread[1:2] - nbr_ticks_ref[b : b + 1, :].astype(F32)
        counts = jnp.broadcast_to(nbr_count_ref[b : b + 1, :].astype(F32), (8, ends)).astype(BF16)
        count = jnp.dot(counts, spread_end, preferred_element_type=F32)[0:1]
        valid = place_in_end < count
        nbr_owner = jnp.where(valid, nbr_owner_ref[b], -1)
        owned_nbr = jnp.where(nbr_owner == peer_col, 1.0, 0.0)
        owned_end = jnp.where(end_owner_ref[b] == peer_col, 1.0, 0.0)
        is_row = jnp.where(iota((node_dev, 1), 0) == nbr_row_ref[b : b + 1, :], 1.0, 0.0).astype(BF16)
        asked = lax.dot_general(owned_nbr.astype(BF16), is_row, NT, preferred_element_type=F32)
        asked = jnp.where(asked > 0.5, 1.0, 0.0)
        slot_of_row, totals = before_each(asked, upper, zero)
        load = jnp.maximum(load, totals)
        nbr_rank = jnp.dot(slot_of_row.astype(BF16), is_row, preferred_element_type=F32)
        nbr_rank = jnp.sum(owned_nbr * nbr_rank, axis=0, keepdims=True)
        nbr_rank = jnp.where(valid, nbr_rank, -1.0)
        rank_ref[b : b + 1, :] = nbr_rank.astype(jnp.int32)
        end_rank, _ = before_each(owned_end, upper, zero)
        end_rank = jnp.sum(owned_end * end_rank, axis=0, keepdims=True)
        slot_ref[b : b + 1, :] = end_owner_ref[b] * CAP_END + end_rank.astype(jnp.int32)
        rank = jnp.concatenate([nbr_rank, end_rank + CAP_NBR], axis=1)
        at_slot = jnp.where(iota((SLOTS, 1), 0).astype(F32) == rank, 1.0, 0.0).astype(BF16)
        owned = jnp.concatenate([owned_nbr, owned_end], axis=1)
        row = jnp.concatenate([nbr_row_ref[b : b + 1, :], end_row_ref[b : b + 1, :]], axis=1)
        named = [(row >> 5).astype(F32), (row & 31).astype(F32), jnp.ones(row.shape, F32)]
        named = jnp.concatenate([(owned * v).astype(BF16) for v in named], axis=0)
        lists = lax.dot_general(named, at_slot, NT, preferred_element_type=F32)
        times = lists[2 * peers : 3 * peers]
        row_id = lists[0:peers] * 32.0 + lists[peers : 2 * peers]
        row_id = jnp.floor(row_id / jnp.maximum(times, 1.0) + 0.5)
        row_id = jnp.where(times > 0.5, row_id, float(node_dev))
        if b == batches - 1:
            most = jnp.max(load, axis=0, keepdims=True)
            row_id = jnp.where(iota((1, SLOTS), 1) == SLOTS - 1, most, row_id)
        ids_ref[:, 0, b * SLOTS : (b + 1) * SLOTS] = row_id.astype(jnp.int32)


def place(node_dev, peers, end_owner, end_row, nbr_owner, nbr_row, event_ticks, nbr_ticks, nbr_count):
    batches, ends = end_row.shape
    nbrs = nbr_row.shape[1]
    return pl.pallas_call(
        functools.partial(place_kernel, node_dev),
        out_shape=(
            jax.ShapeDtypeStruct((peers, 1, batches * SLOTS), jnp.int32),
            jax.ShapeDtypeStruct((batches, nbrs), jnp.int32),
            jax.ShapeDtypeStruct((batches, nbrs), F32),
            jax.ShapeDtypeStruct((batches, ends), jnp.int32),
        ),
        compiler_params=params(),
        cost_estimate=cost(2e9, 1e6),
        name="request_lists",
    )(end_owner, end_row, nbr_owner, nbr_row, event_ticks, nbr_ticks, nbr_count)


def lookup_kernel(start, ranges, asked_ref, rows_ref, found_ref):
    node_dev = rows_ref.shape[0]
    peers, cap, width = found_ref.shape
    ids = asked_ref[:, 0, start : start + SLOTS].T
    ids = jnp.concatenate([ids[lo:hi, :] for lo, hi in ranges], axis=0)
    lane = iota((1, node_dev), 1)
    group = max(1, 512 // cap)
    group = max(g for g in (1, 2, 4, 8, 16, 32) if g <= group)
    for start in range(0, peers, group):
        picks = [
            jnp.where(ids[:, p : p + 1] == lane, 1.0, 0.0).astype(BF16)
            for p in range(start, start + group)
        ]
        picked = jnp.dot(jnp.concatenate(picks, axis=0), rows_ref[...], preferred_element_type=F32)
        found_ref[start : start + group] = picked.astype(BF16).reshape(group, cap, width)


def lookup(batch, ranges, asked, pulled):
    peers = asked.shape[0]
    cap = sum(hi - lo for lo, hi in ranges)
    node_dev, width = pulled.shape
    return pl.pallas_call(
        functools.partial(lookup_kernel, batch * SLOTS, ranges),
        out_shape=jax.ShapeDtypeStruct((peers, cap, width), BF16),
        compiler_params=params(),
        cost_estimate=cost(2 * peers * cap * node_dev * width, 2 * peers * cap * width),
        name="lookup_rows",
    )(asked, pulled)


def ends_kernel(slot_ref, slot_col_ref, pair_col_ref, found_ref, self_ref, push_ref):
    slots = push_ref.shape[0] * push_ref.shape[1]
    width = found_ref.shape[2]
    found = found_ref[...].reshape(slots, width)
    lane = iota((1, slots), 1)
    own = jnp.where(slot_col_ref[...] == lane, 1.0, 0.0).astype(BF16)
    self_ref[...] = jnp.dot(own, found, preferred_element_type=F32).astype(BF16)
    pair = jnp.where(pair_col_ref[...] == lane, 1.0, 0.0).astype(BF16)
    partner = jnp.dot(pair, found, preferred_element_type=F32).astype(BF16)
    to_slot = jnp.where(iota((slots, 1), 0) == slot_ref[...], 1.0, 0.0).astype(BF16)
    push = jnp.dot(to_slot, partner, preferred_element_type=F32).astype(BF16)
    push_ref[...] = push.reshape(push_ref.shape)


def whole(*shape):
    return pl.BlockSpec(shape, lambda g: (0,) * len(shape))


def end_rows(slot, slot_col, pair_col, found):
    ends = slot.shape[1]
    peers, _, width = found.shape
    return pl.pallas_call(
        ends_kernel,
        grid=(1,),
        in_specs=[
            whole(1, ends),
            whole(ends, 1),
            whole(ends, 1),
            whole(peers, CAP_END, width),
        ],
        out_specs=(whole(ends, width), whole(peers, CAP_END, width)),
        out_shape=(
            jax.ShapeDtypeStruct((ends, width), BF16),
            jax.ShapeDtypeStruct((peers, CAP_END, width), BF16),
        ),
        compiler_params=params(),
        cost_estimate=cost(1e9, 2e6),
        name="end_rows",
    )(slot, slot_col, pair_col, found)


def cos_turns(turns):
    part = turns - jnp.floor(turns + 0.5)
    square = part * part
    value = COS_TERMS[-1] * square + COS_TERMS[-2]
    for term in COS_TERMS[-3::-1]:
        value = value * square + term
    return value


def rows_at(at_ref, found_ref):
    peers, held, width = found_ref.shape
    found = found_ref[...].reshape(peers * held, width)
    picks = jnp.where(at_ref[...] == iota((1, peers * held), 1), 1.0, 0.0).astype(BF16)
    return jnp.dot(picks, found, preferred_element_type=F32)


def arrange_kernel(at_ref, found_ref, out_ref):
    out_ref[...] = rows_at(at_ref, found_ref).astype(BF16)


def arrange(at, found):
    nbrs = at.shape[0]
    peers, held, width = found.shape
    return pl.pallas_call(
        arrange_kernel,
        grid=(nbrs // NBR_BLOCK,),
        in_specs=[pl.BlockSpec((NBR_BLOCK, 1), lambda g: (g, 0)), whole(peers, held, width)],
        out_specs=pl.BlockSpec((NBR_BLOCK, width), lambda g: (g, 0)),
        out_shape=jax.ShapeDtypeStruct((nbrs, width), BF16),
        compiler_params=params(),
        cost_estimate=cost(2 * nbrs * peers * held * width, 4 * peers * held * width),
        name="arrange_rows",
    )(at, found)


def attend_kernel(
    at_ref,
    found_ref,
    gap_ref,
    count_ref,
    self_ref,
    turn_ref,
    w_query_ref,
    w_key_value_ref,
    w_out_ref,
    *refs,
):
    out_ref = refs[-1]
    ends, width = self_ref.shape
    nbrs = at_ref.shape[0]
    rows = rows_at(at_ref, found_ref)
    for early_ref in refs[:-1]:
        rows = rows + early_ref[...].astype(F32)
    encoding = cos_turns(gap_ref[...] * turn_ref[0:1, :] + turn_ref[1:2, :])
    keyed = (rows + encoding).astype(BF16)
    query = jnp.dot(self_ref[...], w_query_ref[...], preferred_element_type=F32).astype(BF16)
    packed = jnp.dot(keyed, w_key_value_ref[...], preferred_element_type=F32).astype(BF16)
    place_in_end = iota((ends, nbrs), 1) - NBR * iota((ends, nbrs), 0)
    mine = (place_in_end >= 0) & (place_in_end < count_ref[...])
    scale = 1.0 / math.sqrt(HEAD_DIM)
    parts = []
    for h in range(HEADS):
        lanes = slice(h * HEAD_DIM, (h + 1) * HEAD_DIM)
        score = lax.dot_general(query[:, lanes], packed[:, lanes], NT, preferred_element_type=F32)
        score = jnp.where(mine, score * scale, -1e30)
        raised = jnp.exp(score - jnp.max(score, axis=1, keepdims=True))
        weights = (raised / jnp.sum(raised, axis=1, keepdims=True)).astype(BF16)
        value = packed[:, width + h * HEAD_DIM : width + (h + 1) * HEAD_DIM]
        parts.append(jnp.dot(weights, value, preferred_element_type=F32))
    attended = jnp.concatenate(parts, axis=1).astype(BF16)
    out_ref[...] = self_ref[...].astype(F32) + jnp.dot(
        attended, w_out_ref[...], preferred_element_type=F32
    )


def attend(at, found, gap, count, self_rows, turn, w_query, w_key_value, w_out, early):
    ends, width = self_rows.shape
    nbrs = at.shape[0]
    peers, held, _ = found.shape
    col = pl.BlockSpec((NBR_BLOCK, 1), lambda g: (g, 0))
    end_block = NBR_BLOCK // NBR
    end_spec = pl.BlockSpec((end_block, width), lambda g: (g, 0))
    return pl.pallas_call(
        attend_kernel,
        grid=(nbrs // NBR_BLOCK,),
        in_specs=[
            col,
            whole(peers, held, width),
            col,
            pl.BlockSpec((end_block, 1), lambda g: (g, 0)),
            end_spec,
            whole(8, width),
            whole(width, width),
            whole(width, 2 * width),
            whole(width, width),
        ]
        + [pl.BlockSpec((NBR_BLOCK, width), lambda g: (g, 0)) for _ in early],
        out_specs=end_spec,
        out_shape=jax.ShapeDtypeStruct((ends, width), F32),
        compiler_params=params(),
        cost_estimate=cost(2 * nbrs * width * (peers * held + 2 * width), 4 * nbrs * width),
        name="attend",
    )(at, found, gap, count, self_rows, turn, w_query, w_key_value, w_out, *early)


def gru_kernel(
    order_ref,
    memory_ref,
    ids_ref,
    rows0_ref,
    rows1_ref,
    rows2_ref,
    rows3_ref,
    w_input_ref,
    w_hidden_ref,
    bias_ref,
    *refs,
):
    out_ref, rows_ref, sems = refs[0], refs[-2], refs[-1]
    block, width = memory_ref.shape
    slots = rows0_ref.shape[0]
    step = pl.program_id(0)

    @pl.when(step == 0)
    def _():
        copies = []
        for k, source in enumerate((rows0_ref, rows1_ref, rows2_ref, rows3_ref)):
            at = pl.multiple_of(order_ref[k] * slots, slots)
            copies.append(pltpu.make_async_copy(source, rows_ref.at[pl.ds(at, slots)], sems.at[k]))
        for copy in copies:
            copy.start()
        for copy in copies:
            copy.wait()

    picks = jnp.where(ids_ref[...] == iota((block, 1), 0) + step * block, 1.0, 0.0)
    counts = jnp.sum(picks, axis=1, keepdims=True)
    sums = jnp.dot(picks.astype(BF16), rows_ref[...], preferred_element_type=F32)
    mean = (sums / jnp.maximum(counts, 1.0)).astype(BF16)
    memory = memory_ref[...]
    pulled = memory.astype(BF16)
    dot = functools.partial(jnp.dot, preferred_element_type=F32)
    bias = bias_ref[...]

    own = dot(pulled, w_input_ref[:width, :]) + dot(mean, w_input_ref[width:, :]) + bias
    hidden = dot(pulled, w_hidden_ref[...])
    reset = jax.nn.sigmoid(own[:, :width] + hidden[:, :width])
    update = jax.nn.sigmoid(own[:, width : 2 * width] + hidden[:, width : 2 * width])
    candidate = jnp.tanh(own[:, 2 * width :] + reset * hidden[:, 2 * width :])
    new = jnp.where(counts > 0, (1.0 - update) * candidate + update * memory, memory)
    out_ref[...] = new
    if len(refs) == 4:
        refs[1][...] = new.astype(BF16)


def gru(order, memory, ids, rows, w_input, w_hidden, bias, with_pulled):
    node_dev, width = memory.shape
    slots = rows[0].shape[0]
    block = 512
    anywhere = pl.BlockSpec(memory_space=pl.ANY)
    blocked = pl.BlockSpec((block, width), lambda g: (g, 0))
    types = (F32, BF16) if with_pulled else (F32,)
    return pl.pallas_call(
        gru_kernel,
        grid=(node_dev // block,),
        in_specs=[pl.BlockSpec(memory_space=pltpu.SMEM), blocked, whole(1, 4 * slots)]
        + [anywhere] * 4
        + [whole(2 * width, 3 * width), whole(width, 3 * width), whole(1, 3 * width)],
        out_specs=tuple(blocked for _ in types),
        out_shape=tuple(jax.ShapeDtypeStruct((node_dev, width), t) for t in types),
        scratch_shapes=[pltpu.VMEM((4 * slots, width), BF16), pltpu.SemaphoreType.DMA((4,))],
        compiler_params=params(),
        cost_estimate=cost(8e9, 1e7),
        name="memory_update",
    )(order, memory, ids, *rows, w_input, w_hidden, bias)


def exchange(rows):
    return lax.all_to_all(rows, "nodes", split_axis=0, concat_axis=0, tiled=True)


def after(value, earlier):
    return lax.optimization_barrier((value, earlier))[0]


def across_time(value):
    size = lax.axis_size("tm")
    return [value] + [
        lax.ppermute(value, "tm", [(i, (i + k) % size) for i in range(size)]) for k in range(1, size)
    ]


def shards(
    memory,
    end_owner,
    end_row,
    nbr_owner,
    nbr_row,
    event_ticks,
    nbr_ticks,
    nbr_count,
    time_freq,
    time_phase,
    w_query,
    w_key_value,
    w_out,
    gru_input,
    gru_hidden,
    gru_bias,
):
    peers = lax.axis_size("nodes")
    node_dev, width = memory.shape
    batches, ends = end_row.shape
    ids, rank, gap, slot = place(
        node_dev,
        peers,
        end_owner.transpose(0, 2, 1),
        end_row,
        nbr_owner.transpose(0, 2, 1),
        nbr_row,
        event_ticks,
        nbr_ticks,
        nbr_count,
    )
    asked = exchange(ids)
    end_range = (CAP_NBR, CAP_NBR + CAP_END)
    slot_col = slot[:, :, None]
    pair_col = slot.reshape(batches, -1, 2)[:, :, ::-1].reshape(batches, ends, 1)
    pulled = memory.astype(BF16)

    def ends_of(b, found):
        return end_rows(slot[b : b + 1], slot_col[b], pair_col[b], found)

    found = exchange(lookup(0, (end_range,), asked, pulled))
    self_rows, push = ends_of(0, found)
    arrived = exchange(push)

    arrived_ids = asked.reshape(peers, batches, SLOTS)[:, :, CAP_NBR : CAP_NBR + CAP_END]
    arrived_ids = arrived_ids.transpose(1, 0, 2).reshape(batches, peers * CAP_END)
    load = jnp.broadcast_to(jnp.max(asked[:, 0, -1]), (1, peers * CAP_END))
    here = lax.axis_index("tm")
    order = jnp.mod(here - jnp.arange(4, dtype=jnp.int32), 4)
    shared = jnp.stack(across_time(jnp.concatenate([arrived_ids, load])))
    most = jnp.max(shared[:, batches])
    all_ids = shared[order].transpose(1, 0, 2).reshape(batches + 1, 1, 4 * peers * CAP_END)

    turn = jnp.stack([time_freq, time_phase]) * (1.0 / (2.0 * math.pi))
    turn = jnp.concatenate([turn, jnp.zeros((6, width), F32)])
    bias = gru_bias[None, :]
    gap_col, count_col = gap[:, :, None], nbr_count[:, :, None]

    def finish(cap, early):
        def at(b, lo, hi, skip):
            held = hi - lo + skip
            inside = (rank[b] >= lo) & (rank[b] < hi)
            return jnp.where(inside, nbr_owner[b, :, 0] * held + skip + rank[b] - lo, -1)[:, None]

        def attention(b, where, found, rows, parts):
            return attend(
                where, found, gap_col[b], count_col[b], rows, turn, w_query, w_key_value, w_out, parts
            )

        def update(b, state, arrived, with_pulled):
            rows = across_time(arrived.reshape(peers * CAP_END, width))
            return gru(order, state, all_ids[b], rows, gru_input, gru_hidden, bias, with_pulled)

        found = exchange(after(lookup(0, ((0, cap),), asked, pulled), arrived))
        state, pulled_next = update(0, memory, arrived, True)
        first = attention(0, at(0, 0, cap, 0), found, self_rows, ())
        found = exchange(after(lookup(1, (end_range, (0, early)), asked, pulled_next), found))
        rows_next, push = ends_of(1, found)
        arrived_next = exchange(push)
        part = arrange(at(1, 0, early, CAP_END), found)
        found = exchange(after(lookup(1, ((early, cap),), asked, pulled_next), arrived_next))
        (state,) = update(1, state, arrived_next, False)
        second = attention(1, at(1, early, cap, 0), found, rows_next, (part,))
        return jnp.stack([first, second]), state

    return lax.cond(
        most <= CAP_FAST,
        functools.partial(finish, CAP_FAST, CAP_EARLY),
        functools.partial(finish, CAP_NBR, CAP_NBR // 2),
    )


def solution(mesh):
    return jax.shard_map(
        shards,
        mesh=mesh,
        in_specs=(
            P("nodes", None),
            P(None, ("nodes", "tm"), None),
            P(None, ("nodes", "tm")),
            P(None, ("nodes", "tm"), None),
            P(None, ("nodes", "tm")),
            P(None, ("nodes", "tm")),
            P(None, ("nodes", "tm")),
            P(None, ("nodes", "tm")),
            P(),
            P(),
            P(),
            P(),
            P(),
            P(),
            P(),
            P(),
        ),
        out_specs=(P(None, ("nodes", "tm"), None), P("nodes", None)),
        check_vma=False,
    )
```

```python
import functools
import math

import jax
import jax.numpy as jnp
import numpy as np
from jax import lax
from jax.experimental import pallas as pl
from jax.experimental.pallas import tpu as pltpu
from jax.sharding import PartitionSpec as P

HEADS = 4
NBR = 10
HEAD_DIM = 128
CAP_END = 16
CAP_NBR = 160
SLOTS = 256
CAP_FAST = 80
CAP_EARLY = 48
UPDATE_BLOCK = 256
NBR_BLOCK = 640
F32 = jnp.float32
BF16 = jnp.bfloat16
VMEM_LIMIT = 56 * 1024 * 1024
NT = (((1,), (1,)), ((), ()))
COS_TERMS = tuple(
    np.polynomial.chebyshev.Chebyshev.interpolate(
        lambda u: np.cos(2 * np.pi * np.sqrt(u)), 7, domain=[0.0, 0.25]
    )
    .convert(kind=np.polynomial.Polynomial)
    .coef.tolist()
)


def params(steps=None):
    return pltpu.CompilerParams(vmem_limit_bytes=VMEM_LIMIT)


def cost(flops, size):
    return pl.CostEstimate(flops=int(flops), bytes_accessed=int(size), transcendentals=0)


def iota(shape, dim):
    return lax.broadcasted_iota(jnp.int32, shape, dim)


def whole(*shape):
    return pl.BlockSpec(shape, lambda g: (0,) * len(shape))


def one_hot(mask):
    return jnp.where(mask, 1.0, 0.0).astype(BF16)


def dot(left, right):
    return jnp.dot(left, right, preferred_element_type=F32)


def dot_nt(left, right):
    return lax.dot_general(left, right, NT, preferred_element_type=F32)


def columns(*rows):
    size = rows[0].shape[1]
    rows = [row.astype(F32) for row in rows]
    turned = jnp.concatenate(rows + [jnp.zeros((8 - len(rows), size), F32)], axis=0).T
    return [turned[:, i : i + 1] for i in range(len(rows))]


def place_kernel(
    node_dev,
    end_owner_ref,
    end_row_ref,
    nbr_owner_ref,
    nbr_row_ref,
    event_ticks_ref,
    nbr_ticks_ref,
    nbr_count_ref,
    ids_ref,
    rank_ref,
    gap_ref,
    slot_ref,
):
    batches, ends = end_row_ref.shape
    nbrs = nbr_row_ref.shape[1]
    peers = ids_ref.shape[0]
    lows = 128
    highs = node_dev // lows
    upper = one_hot(iota((ends, ends), 0) < iota((ends, ends), 1))
    group, other = iota((peers * highs, peers * highs), 0), iota((peers * highs, peers * highs), 1)
    earlier = one_hot((other < group) & (other >= group - (group & (highs - 1))))
    lane_e = iota((ends // 2, nbrs), 1) - 2 * NBR * iota((ends // 2, nbrs), 0)
    spread_event = one_hot((lane_e >= 0) & (lane_e < 2 * NBR))
    lane_n = iota((ends, nbrs), 1) - NBR * iota((ends, nbrs), 0)
    spread_end = one_hot((lane_n >= 0) & (lane_n < NBR))
    lane = iota((1, nbrs), 1)
    place_in_end = lane - NBR * jnp.floor((lane.astype(F32) + 0.5) * (1.0 / NBR)).astype(jnp.int32)
    row8 = iota((8, 1), 0)
    peer_col = iota((peers, 1), 0)
    load = jnp.zeros((peers * highs, 1), F32)
    for b in range(batches):
        ticks = event_ticks_ref[b : b + 1, :]
        halves = jnp.where(row8 == 0, ticks >> 7, ticks & 127).astype(F32).astype(BF16)
        spread = dot(halves, spread_event)
        gap_ref[b : b + 1, :] = spread[0:1] * 128.0 + spread[1:2] - nbr_ticks_ref[b : b + 1, :].astype(F32)
        counts = jnp.broadcast_to(nbr_count_ref[b : b + 1, :].astype(F32), (8, ends)).astype(BF16)
        valid = place_in_end.astype(F32) < dot(counts, spread_end)[0:1]
        nbr_owner = jnp.where(valid, nbr_owner_ref[b], -1)
        nbr_row = nbr_row_ref[b : b + 1, :]
        owned_nbr = jnp.where(nbr_owner == peer_col, 1.0, 0.0)
        owned_end = jnp.where(end_owner_ref[b] == peer_col, 1.0, 0.0)
        in_group = jnp.where(nbr_owner * highs + (nbr_row >> 7) == iota((peers * highs, 1), 0), 1.0, 0.0)
        is_low = one_hot((nbr_row & (lows - 1)) == iota((lows, 1), 0))
        asked = jnp.where(dot_nt(in_group.astype(BF16), is_low) > 0.5, 1.0, 0.0)
        totals = jnp.broadcast_to(jnp.sum(asked, axis=1, keepdims=True), asked.shape)
        offset = dot(earlier, totals.astype(BF16))
        load = jnp.maximum(load, (offset + totals)[:, 0:1])
        slot_of_row = dot(asked.astype(BF16), upper[:lows, :lows]) + offset
        nbr_rank = jnp.sum(in_group * dot(slot_of_row.astype(BF16), is_low), axis=0, keepdims=True)
        nbr_rank = jnp.where(valid, nbr_rank, -1.0)
        rank_ref[b : b + 1, :] = nbr_rank.astype(jnp.int32)
        end_rank = jnp.sum(owned_end * dot(owned_end.astype(BF16), upper), axis=0, keepdims=True)
        slot_ref[b : b + 1, :] = end_owner_ref[b] * CAP_END + end_rank.astype(jnp.int32)
        rank = jnp.concatenate([nbr_rank, end_rank + CAP_NBR], axis=1)
        at_slot = one_hot(iota((SLOTS, 1), 0).astype(F32) == rank)
        owned = jnp.concatenate([owned_nbr, owned_end], axis=1)
        row = jnp.concatenate([nbr_row, end_row_ref[b : b + 1, :]], axis=1)
        named = [(row >> 5).astype(F32), (row & 31).astype(F32), jnp.ones(row.shape, F32)]
        named = jnp.concatenate([(owned * v).astype(BF16) for v in named], axis=0)
        lists = dot_nt(named, at_slot)
        times = lists[2 * peers : 3 * peers]
        row_id = lists[0:peers] * 32.0 + lists[peers : 2 * peers]
        row_id = jnp.floor(row_id / jnp.maximum(times, 1.0) + 0.5)
        row_id = jnp.where(times > 0.5, row_id, float(node_dev))
        if b == batches - 1:
            most = jnp.max(load, axis=0, keepdims=True)
            row_id = jnp.where(iota((1, SLOTS), 1) == SLOTS - 1, most, row_id)
        ids_ref[:, 0, b * SLOTS : (b + 1) * SLOTS] = row_id.astype(jnp.int32)


def place(node_dev, peers, end_owner, end_row, nbr_owner, nbr_row, event_ticks, nbr_ticks, nbr_count):
    batches, ends = end_row.shape
    nbrs = nbr_row.shape[1]
    return pl.pallas_call(
        functools.partial(place_kernel, node_dev),
        out_shape=(
            jax.ShapeDtypeStruct((peers, 1, batches * SLOTS), jnp.int32),
            jax.ShapeDtypeStruct((batches, nbrs), jnp.int32),
            jax.ShapeDtypeStruct((batches, nbrs), F32),
            jax.ShapeDtypeStruct((batches, ends), jnp.int32),
        ),
        compiler_params=params(),
        cost_estimate=cost(2e9, 1e6),
        name="request_lists",
    )(end_owner, end_row, nbr_owner, nbr_row, event_ticks, nbr_ticks, nbr_count)


def lookup_kernel(start, ranges, asked_ref, rows_ref, found_ref):
    node_dev = rows_ref.shape[0]
    peers, cap, width = found_ref.shape
    ids = asked_ref[:, 0, start : start + SLOTS].T
    ids = jnp.concatenate([ids[lo:hi, :] for lo, hi in ranges], axis=0)
    lane = iota((1, node_dev), 1)
    group = max(1, 512 // cap)
    group = max(g for g in (1, 2, 4, 8, 16, 32) if g <= group)
    for start in range(0, peers, group):
        picks = [
            one_hot(ids[:, p : p + 1] == lane)
            for p in range(start, start + group)
        ]
        picked = dot(jnp.concatenate(picks, axis=0), rows_ref[...])
        found_ref[start : start + group] = picked.astype(BF16).reshape(group, cap, width)


def lookup(batch, ranges, asked, pulled):
    peers = asked.shape[0]
    cap = sum(hi - lo for lo, hi in ranges)
    node_dev, width = pulled.shape
    return pl.pallas_call(
        functools.partial(lookup_kernel, batch * SLOTS, ranges),
        out_shape=jax.ShapeDtypeStruct((peers, cap, width), BF16),
        compiler_params=params(),
        cost_estimate=cost(2 * peers * cap * node_dev * width, 2 * peers * cap * width),
        name="lookup_rows",
    )(asked, pulled)


def ends_kernel(batch, slot_ref, found_ref, self_ref, push_ref):
    ends, width = self_ref.shape
    slots = push_ref.shape[0] * push_ref.shape[1]
    found = found_ref[...].reshape(slots, width)
    slot = slot_ref[batch : batch + 1, :]
    own = dot(one_hot(columns(slot)[0].astype(jnp.int32) == iota((1, slots), 1)), found).astype(BF16)
    self_ref[...] = own
    swap = one_hot((iota((ends, 1), 0) ^ 1) == iota((1, ends), 1))
    push = dot(one_hot(iota((slots, 1), 0) == slot), dot(swap, own).astype(BF16))
    push_ref[...] = push.astype(BF16).reshape(push_ref.shape)


def end_rows(batch, slot, found):
    batches, ends = slot.shape
    peers, _, width = found.shape
    return pl.pallas_call(
        functools.partial(ends_kernel, batch),
        grid=(1,),
        in_specs=[whole(batches, ends), whole(peers, CAP_END, width)],
        out_specs=(whole(ends, width), whole(peers, CAP_END, width)),
        out_shape=(
            jax.ShapeDtypeStruct((ends, width), BF16),
            jax.ShapeDtypeStruct((peers, CAP_END, width), BF16),
        ),
        compiler_params=params(),
        cost_estimate=cost(1e9, 2e6),
        name="end_rows",
    )(slot, found)


def cos_turns(turns):
    part = turns - jnp.floor(turns + 0.5)
    square = part * part
    value = COS_TERMS[-1] * square + COS_TERMS[-2]
    for term in COS_TERMS[-3::-1]:
        value = value * square + term
    return value


def answer_index(batch, span, owner_ref, rank_ref, held):
    lo, hi = span
    rank = rank_ref[batch : batch + 1, :]
    index = owner_ref[batch] * held + (held - hi) + rank
    return jnp.where((rank >= lo) & (rank < hi), index, -1)


def rows_at(index, found_ref):
    peers, held, width = found_ref.shape
    picks = one_hot(index.astype(jnp.int32) == iota((1, peers * held), 1))
    return dot(picks, found_ref[...].reshape(peers * held, width))


def arrange_kernel(batch, span, owner_ref, rank_ref, found_ref, out_ref):
    (index,) = columns(answer_index(batch, span, owner_ref, rank_ref, found_ref.shape[1]))
    out_ref[...] = rows_at(index, found_ref).astype(BF16)


def neighbour_specs(batches):
    return [
        pl.BlockSpec((batches, 1, NBR_BLOCK), lambda g: (0, 0, g)),
        pl.BlockSpec((batches, NBR_BLOCK), lambda g: (0, g)),
    ]


def arrange(batch, span, owner, rank, found):
    batches, nbrs = rank.shape
    peers, held, width = found.shape
    return pl.pallas_call(
        functools.partial(arrange_kernel, batch, span),
        grid=(nbrs // NBR_BLOCK,),
        in_specs=neighbour_specs(batches) + [whole(peers, held, width)],
        out_specs=pl.BlockSpec((NBR_BLOCK, width), lambda g: (g, 0)),
        out_shape=jax.ShapeDtypeStruct((nbrs, width), BF16),
        compiler_params=params(),
        cost_estimate=cost(2 * nbrs * peers * held * width, 4 * peers * held * width),
        name="arrange_rows",
    )(owner, rank, found)


def attend_kernel(
    batch,
    span,
    owner_ref,
    rank_ref,
    gap_ref,
    found_ref,
    self_ref,
    turn_ref,
    w_query_ref,
    w_key_value_ref,
    w_out_ref,
    *refs,
):
    out_ref = refs[-1]
    ends, width = self_ref.shape
    nbrs = rank_ref.shape[1]
    index = answer_index(batch, span, owner_ref, rank_ref, found_ref.shape[1])
    index, gap = columns(index, gap_ref[batch : batch + 1, :])
    rows = rows_at(index, found_ref)
    if batch:
        rows = rows + refs[0][...].astype(F32)
    encoding = cos_turns(gap * turn_ref[0:1, :] + turn_ref[1:2, :])
    keyed = (rows + encoding).astype(BF16)
    packed = dot(keyed, w_key_value_ref[...]).astype(BF16)
    query = dot(self_ref[...], w_query_ref[...])
    head = iota((1, width), 1) // HEAD_DIM
    queries = [jnp.where(head == h, query, 0.0).astype(BF16) for h in range(HEADS)]
    score = dot_nt(jnp.concatenate(queries, axis=0), packed[:, :width]) * (1.0 / math.sqrt(HEAD_DIM))
    end = iota((HEADS * ends, 1), 0) & (ends - 1)
    place_in_end = iota((1, nbrs), 1) - NBR * end
    mine = (place_in_end >= 0) & (place_in_end < NBR) & (rank_ref[batch : batch + 1, :] >= 0)
    score = jnp.where(mine, score, -1e30)
    raised = jnp.exp(score - jnp.max(score, axis=1, keepdims=True))
    weights = (raised / jnp.sum(raised, axis=1, keepdims=True)).astype(BF16)
    mixed = dot(weights, packed[:, width:])
    attended = [
        mixed[h * ends : (h + 1) * ends, h * HEAD_DIM : (h + 1) * HEAD_DIM] for h in range(HEADS)
    ]
    attended = jnp.concatenate(attended, axis=1).astype(BF16)
    out_ref[0] = self_ref[...].astype(F32) + dot(attended, w_out_ref[...])


def attend(batch, span, owner, rank, gap, found, self_rows, turn, weights, earlier):
    ends, width = self_rows.shape
    batches, nbrs = rank.shape
    peers, held, _ = found.shape
    end_block = NBR_BLOCK // NBR
    specs = neighbour_specs(batches) + [
        pl.BlockSpec((batches, NBR_BLOCK), lambda g: (0, g)),
        whole(peers, held, width),
        pl.BlockSpec((end_block, width), lambda g: (g, 0)),
        whole(8, width),
        whole(width, width),
        whole(width, 2 * width),
        whole(width, width),
    ]
    aliases = {}
    if earlier:
        aliases = {len(specs) + 1: 0}
        specs += [
            pl.BlockSpec((NBR_BLOCK, width), lambda g: (g, 0)),
            pl.BlockSpec(memory_space=pl.ANY),
        ]
    return pl.pallas_call(
        functools.partial(attend_kernel, batch, span),
        grid=(nbrs // NBR_BLOCK,),
        in_specs=specs,
        out_specs=pl.BlockSpec((1, end_block, width), lambda g: (batch, g, 0)),
        out_shape=jax.ShapeDtypeStruct((batches, ends, width), F32),
        input_output_aliases=aliases,
        compiler_params=params(),
        cost_estimate=cost(2 * nbrs * width * (peers * held + 2 * width), 4 * nbrs * width),
        name="attend",
    )(owner, rank, gap, found, self_rows, turn, *weights, *earlier)


def project_kernel(memory_ref, w_input_ref, w_hidden_ref, bias_ref, out_ref):
    width = memory_ref.shape[1]
    pulled = memory_ref[...].astype(BF16)
    own = dot(pulled, w_input_ref[...]) + bias_ref[...]
    hidden = dot(pulled, w_hidden_ref[...])
    out_ref[:, : 2 * width] = own[:, : 2 * width] + hidden[:, : 2 * width]
    out_ref[:, 2 * width : 3 * width] = own[:, 2 * width :]
    out_ref[:, 3 * width :] = hidden[:, 2 * width :]


def project(memory, w_input, w_hidden, bias):
    node_dev, width = memory.shape
    block = 512
    return pl.pallas_call(
        project_kernel,
        grid=(node_dev // block,),
        in_specs=[
            pl.BlockSpec((block, width), lambda g: (g, 0)),
            whole(width, 3 * width),
            whole(width, 3 * width),
            whole(1, 3 * width),
        ],
        out_specs=pl.BlockSpec((block, 4 * width), lambda g: (g, 0)),
        out_shape=jax.ShapeDtypeStruct((node_dev, 4 * width), F32),
        compiler_params=params(),
        cost_estimate=cost(4 * node_dev * width * 3 * width, 12e6),
        name="project_memory",
    )(memory, w_input, w_hidden, bias)


def update_kernel(
    order_ref,
    memory_ref,
    own_ref,
    ids_ref,
    rows0_ref,
    rows1_ref,
    rows2_ref,
    rows3_ref,
    w_message_ref,
    *refs,
):
    rows_ref, sems = refs[-2:]
    block, width = memory_ref.shape
    slots = rows0_ref.shape[0]
    step = pl.program_id(0)

    @pl.when(step == 0)
    def _():
        copies = []
        for k, source in enumerate((rows0_ref, rows1_ref, rows2_ref, rows3_ref)):
            at = pl.multiple_of(order_ref[k] * slots, slots)
            copies.append(pltpu.make_async_copy(source, rows_ref.at[pl.ds(at, slots)], sems.at[k]))
        for copy in copies:
            copy.start()
        for copy in copies:
            copy.wait()

    picks = jnp.where(ids_ref[...] == iota((block, 1), 0) + step * block, 1.0, 0.0)
    counts = jnp.sum(picks, axis=1, keepdims=True)
    mean = dot(picks.astype(BF16), rows_ref[...]) / jnp.maximum(counts, 1.0)
    gates = dot(mean.astype(BF16), w_message_ref[...])
    memory = memory_ref[...]
    reset = jax.nn.sigmoid(own_ref[:, :width] + gates[:, :width])
    update = jax.nn.sigmoid(own_ref[:, width : 2 * width] + gates[:, width : 2 * width])
    hidden = own_ref[:, 3 * width :]
    candidate = jnp.tanh(own_ref[:, 2 * width : 3 * width] + gates[:, 2 * width :] + reset * hidden)
    new = jnp.where(counts > 0, (1.0 - update) * candidate + update * memory, memory)
    refs[0][...] = new
    if len(refs) == 4:
        refs[1][...] = new.astype(BF16)


def update_memory(order, memory, own, ids, rows, w_input, with_pulled):
    node_dev, width = memory.shape
    slots = rows[0].shape[0]
    block = UPDATE_BLOCK
    anywhere = pl.BlockSpec(memory_space=pl.ANY)
    blocked = pl.BlockSpec((block, width), lambda g: (g, 0))
    types = (F32, BF16) if with_pulled else (F32,)
    return pl.pallas_call(
        update_kernel,
        grid=(node_dev // block,),
        in_specs=[
            pl.BlockSpec(memory_space=pltpu.SMEM),
            blocked,
            pl.BlockSpec((block, 4 * width), lambda g: (g, 0)),
            whole(1, 4 * slots),
        ]
        + [anywhere] * 4
        + [pl.BlockSpec((width, 3 * width), lambda g: (1, 0))],
        out_specs=tuple(blocked for _ in types),
        out_shape=tuple(jax.ShapeDtypeStruct((node_dev, width), t) for t in types),
        scratch_shapes=[pltpu.VMEM((4 * slots, width), BF16), pltpu.SemaphoreType.DMA((4,))],
        compiler_params=params(),
        cost_estimate=cost(4e9, 1e7),
        name="memory_update",
    )(order, memory, own, ids, *rows, w_input)


def exchange(rows):
    return lax.all_to_all(rows, "nodes", split_axis=0, concat_axis=0, tiled=True)


def after(value, earlier):
    return lax.optimization_barrier((value, earlier))[0]


def across_time(value):
    size = lax.axis_size("tm")
    return [value] + [
        lax.ppermute(value, "tm", [(i, (i + k) % size) for i in range(size)]) for k in range(1, size)
    ]


def shards(
    memory,
    end_owner,
    end_row,
    nbr_owner,
    nbr_row,
    event_ticks,
    nbr_ticks,
    nbr_count,
    time_freq,
    time_phase,
    w_query,
    w_key_value,
    w_out,
    gru_input,
    gru_hidden,
    gru_bias,
):
    peers = lax.axis_size("nodes")
    node_dev, width = memory.shape
    batches = end_row.shape[0]
    end_owner, nbr_owner = end_owner.transpose(0, 2, 1), nbr_owner.transpose(0, 2, 1)
    ids, rank, gap, slot = place(
        node_dev, peers, end_owner, end_row, nbr_owner, nbr_row, event_ticks, nbr_ticks, nbr_count
    )
    asked = exchange(ids)
    end_range = (CAP_NBR, CAP_NBR + CAP_END)
    pulled = memory.astype(BF16)
    found = exchange(lookup(0, (end_range,), asked, pulled))
    self_rows, push = end_rows(0, slot, found)
    arrived = exchange(push)

    arrived_ids = asked.reshape(peers, batches, SLOTS)[:, :, CAP_NBR : CAP_NBR + CAP_END]
    arrived_ids = arrived_ids.transpose(1, 0, 2).reshape(batches, peers * CAP_END)
    load = jnp.broadcast_to(jnp.max(asked[:, 0, -1]), (1, peers * CAP_END))
    here = lax.axis_index("tm")
    order = jnp.mod(here - jnp.arange(4, dtype=jnp.int32), 4)
    shared = jnp.stack(across_time(jnp.concatenate([arrived_ids, load])))
    most = jnp.max(shared[:, batches])
    all_ids = shared[order].transpose(1, 0, 2).reshape(batches + 1, 1, 4 * peers * CAP_END)

    turn = jnp.stack([time_freq, time_phase]) * (1.0 / (2.0 * math.pi))
    turn = jnp.concatenate([turn, jnp.zeros((6, width), F32)])
    bias = gru_bias[None, :]
    weights = (w_query, w_key_value, w_out)

    def window(cap, early):
        def update(b, state, arrived, with_pulled):
            own = project(state, gru_input, gru_hidden, bias)
            rows = across_time(arrived.reshape(peers * CAP_END, width))
            return update_memory(order, state, own, all_ids[b], rows, gru_input, with_pulled)

        found = exchange(after(lookup(0, ((0, cap),), asked, pulled), arrived))
        state, pulled_next = update(0, memory, arrived, True)
        embedded = attend(0, (0, cap), nbr_owner, rank, gap, found, self_rows, turn, weights, ())
        found = exchange(after(lookup(1, (end_range, (0, early)), asked, pulled_next), found))
        found, embedded = lax.optimization_barrier((found, embedded))
        rows_next, push = end_rows(1, slot, found)
        arrived_next = exchange(push)
        part = arrange(1, (0, early), nbr_owner, rank, found)
        found = exchange(after(lookup(1, ((early, cap),), asked, pulled_next), arrived_next))
        (state,) = update(1, state, arrived_next, False)
        embedded = attend(
            1, (early, cap), nbr_owner, rank, gap, found, rows_next, turn, weights, (part, embedded)
        )
        return embedded, state

    short = window(CAP_FAST, CAP_EARLY)
    return lax.cond(
        most <= CAP_FAST, lambda done: done, lambda done: window(CAP_NBR, CAP_NBR // 2), short
    )


def solution(mesh):
    return jax.shard_map(
        shards,
        mesh=mesh,
        in_specs=(
            P("nodes", None),
            P(None, ("nodes", "tm"), None),
            P(None, ("nodes", "tm")),
            P(None, ("nodes", "tm"), None),
            P(None, ("nodes", "tm")),
            P(None, ("nodes", "tm")),
            P(None, ("nodes", "tm")),
            P(None, ("nodes", "tm")),
            P(),
            P(),
            P(),
            P(),
            P(),
            P(),
            P(),
            P(),
        ),
        out_specs=(P(None, ("nodes", "tm"), None), P("nodes", None)),
        check_vma=False,
    )
```

```python
import functools
import math

import jax
import jax.numpy as jnp
import numpy as np
from jax import lax
from jax.experimental import pallas as pl
from jax.experimental.pallas import tpu as pltpu
from jax.sharding import PartitionSpec as P

HEADS = 4
NBR = 10
HEAD_DIM = 128
CAP_END = 16
CAP_NBR = 160
SLOTS = 256
CAP_FAST = 80
UPDATE_BLOCK = 256
NBR_BLOCK = 640
F32 = jnp.float32
BF16 = jnp.bfloat16
NT = (((1,), (1,)), ((), ()))
COS_TERMS = tuple(
    np.polynomial.chebyshev.Chebyshev.interpolate(
        lambda u: np.cos(2 * np.pi * np.sqrt(u)), 7, domain=[0.0, 0.25]
    )
    .convert(kind=np.polynomial.Polynomial)
    .coef.tolist()
)


def params(mib):
    return pltpu.CompilerParams(vmem_limit_bytes=mib * 1024 * 1024)


def cost(flops, size):
    return pl.CostEstimate(flops=int(flops), bytes_accessed=int(size), transcendentals=0)


def iota(shape, dim):
    return lax.broadcasted_iota(jnp.int32, shape, dim)


def whole(*shape):
    return pl.BlockSpec(shape, lambda g: (0,) * len(shape))


def one_hot(mask):
    return jnp.where(mask, 1.0, 0.0).astype(BF16)


def dot(left, right):
    return jnp.dot(left, right, preferred_element_type=F32)


def dot_nt(left, right):
    return lax.dot_general(left, right, NT, preferred_element_type=F32)


def columns(*rows):
    size = rows[0].shape[1]
    rows = [row.astype(F32) for row in rows]
    turned = jnp.concatenate(rows + [jnp.zeros((8 - len(rows), size), F32)], axis=0).T
    return [turned[:, i : i + 1] for i in range(len(rows))]


def place_kernel(
    node_dev,
    end_owner_ref,
    end_row_ref,
    nbr_owner_ref,
    nbr_row_ref,
    event_ticks_ref,
    nbr_ticks_ref,
    nbr_count_ref,
    ids_ref,
    rank_ref,
    gap_ref,
    slot_ref,
):
    batches, ends = end_row_ref.shape
    nbrs = nbr_row_ref.shape[1]
    peers = ids_ref.shape[0]
    lows = 128
    highs = node_dev // lows
    upper = one_hot(iota((ends, ends), 0) < iota((ends, ends), 1))
    group, other = iota((peers * highs, peers * highs), 0), iota((peers * highs, peers * highs), 1)
    earlier = one_hot((other < group) & (other >= group - (group & (highs - 1))))
    lane_e = iota((ends // 2, nbrs), 1) - 2 * NBR * iota((ends // 2, nbrs), 0)
    spread_event = one_hot((lane_e >= 0) & (lane_e < 2 * NBR))
    lane_n = iota((ends, nbrs), 1) - NBR * iota((ends, nbrs), 0)
    spread_end = one_hot((lane_n >= 0) & (lane_n < NBR))
    lane = iota((1, nbrs), 1)
    place_in_end = lane - NBR * jnp.floor((lane.astype(F32) + 0.5) * (1.0 / NBR)).astype(jnp.int32)
    row8 = iota((8, 1), 0)
    peer_col = iota((peers, 1), 0)
    load = jnp.zeros((peers * highs, 1), F32)
    for b in range(batches):
        ticks = event_ticks_ref[b : b + 1, :]
        halves = jnp.where(row8 == 0, ticks >> 7, ticks & 127).astype(F32).astype(BF16)
        spread = dot(halves, spread_event)
        gap_ref[b : b + 1, :] = spread[0:1] * 128.0 + spread[1:2] - nbr_ticks_ref[b : b + 1, :].astype(F32)
        counts = jnp.broadcast_to(nbr_count_ref[b : b + 1, :].astype(F32), (8, ends)).astype(BF16)
        valid = place_in_end.astype(F32) < dot(counts, spread_end)[0:1]
        nbr_owner = jnp.where(valid, nbr_owner_ref[b], -1)
        nbr_row = nbr_row_ref[b : b + 1, :]
        owned_nbr = jnp.where(nbr_owner == peer_col, 1.0, 0.0)
        owned_end = jnp.where(end_owner_ref[b] == peer_col, 1.0, 0.0)
        in_group = jnp.where(nbr_owner * highs + (nbr_row >> 7) == iota((peers * highs, 1), 0), 1.0, 0.0)
        is_low = one_hot((nbr_row & (lows - 1)) == iota((lows, 1), 0))
        asked = jnp.where(dot_nt(in_group.astype(BF16), is_low) > 0.5, 1.0, 0.0)
        totals = jnp.broadcast_to(jnp.sum(asked, axis=1, keepdims=True), asked.shape)
        offset = dot(earlier, totals.astype(BF16))
        load = jnp.maximum(load, (offset + totals)[:, 0:1])
        slot_of_row = dot(asked.astype(BF16), upper[:lows, :lows]) + offset
        nbr_rank = jnp.sum(in_group * dot(slot_of_row.astype(BF16), is_low), axis=0, keepdims=True)
        nbr_rank = jnp.where(valid, nbr_rank, -1.0)
        rank_ref[b : b + 1, :] = nbr_rank.astype(jnp.int32)
        end_rank = jnp.sum(owned_end * dot(owned_end.astype(BF16), upper), axis=0, keepdims=True)
        slot_ref[b : b + 1, :] = end_owner_ref[b] * CAP_END + end_rank.astype(jnp.int32)
        rank = jnp.concatenate([nbr_rank, end_rank + CAP_NBR], axis=1)
        at_slot = one_hot(iota((SLOTS, 1), 0).astype(F32) == rank)
        owned = jnp.concatenate([owned_nbr, owned_end], axis=1)
        row = jnp.concatenate([nbr_row, end_row_ref[b : b + 1, :]], axis=1)
        named = [(row >> 5).astype(F32), (row & 31).astype(F32), jnp.ones(row.shape, F32)]
        named = jnp.concatenate([(owned * v).astype(BF16) for v in named], axis=0)
        lists = dot_nt(named, at_slot)
        times = lists[2 * peers : 3 * peers]
        row_id = lists[0:peers] * 32.0 + lists[peers : 2 * peers]
        row_id = jnp.floor(row_id / jnp.maximum(times, 1.0) + 0.5)
        row_id = jnp.where(times > 0.5, row_id, float(node_dev))
        if b == batches - 1:
            most = jnp.max(load, axis=0, keepdims=True)
            row_id = jnp.where(iota((1, SLOTS), 1) == SLOTS - 1, most, row_id)
        ids_ref[:, 0, b * SLOTS : (b + 1) * SLOTS] = row_id.astype(jnp.int32)


def place(node_dev, peers, end_owner, end_row, nbr_owner, nbr_row, event_ticks, nbr_ticks, nbr_count):
    batches, ends = end_row.shape
    nbrs = nbr_row.shape[1]
    return pl.pallas_call(
        functools.partial(place_kernel, node_dev),
        out_shape=(
            jax.ShapeDtypeStruct((peers, 1, batches * SLOTS), jnp.int32),
            jax.ShapeDtypeStruct((batches, nbrs), jnp.int32),
            jax.ShapeDtypeStruct((batches, nbrs), F32),
            jax.ShapeDtypeStruct((batches, ends), jnp.int32),
        ),
        compiler_params=params(60),
        cost_estimate=cost(2e9, 1e6),
        name="request_lists",
    )(end_owner, end_row, nbr_owner, nbr_row, event_ticks, nbr_ticks, nbr_count)


def lookup_kernel(start, ranges, asked_ref, rows_ref, found_ref):
    node_dev = rows_ref.shape[0]
    peers, cap, width = found_ref.shape
    ids = asked_ref[:, 0, start : start + SLOTS].T
    ids = jnp.concatenate([ids[lo:hi, :] for lo, hi in ranges], axis=0)
    lane = iota((1, node_dev), 1)
    rows = rows_ref[...].astype(BF16)
    group = max(1, 512 // cap)
    group = max(g for g in (1, 2, 4, 8, 16, 32) if g <= group)
    for start in range(0, peers, group):
        picks = [
            one_hot(ids[:, p : p + 1] == lane)
            for p in range(start, start + group)
        ]
        picked = dot(jnp.concatenate(picks, axis=0), rows)
        found_ref[start : start + group] = picked.astype(BF16).reshape(group, cap, width)


def lookup(batch, ranges, asked, pulled):
    peers = asked.shape[0]
    cap = sum(hi - lo for lo, hi in ranges)
    node_dev, width = pulled.shape
    return pl.pallas_call(
        functools.partial(lookup_kernel, batch * SLOTS, ranges),
        out_shape=jax.ShapeDtypeStruct((peers, cap, width), BF16),
        compiler_params=params(24),
        cost_estimate=cost(2 * peers * cap * node_dev * width, 2 * peers * cap * width),
        name="lookup_rows",
    )(asked, pulled)


def push_kernel(batch, slot_ref, found_ref, push_ref):
    ends = slot_ref.shape[1]
    peers, held, width = found_ref.shape
    slots = peers * held
    slot = slot_ref[batch : batch + 1, :]
    after_lane, before_lane = pltpu.roll(slot, ends - 1, 1), pltpu.roll(slot, 1, 1)
    partner = jnp.where((iota((1, ends), 1) & 1) == 0, after_lane, before_lane)
    sent = iota((slots, 1), 0) == slot
    source = jnp.sum(jnp.where(sent, partner + 1, 0).astype(F32), axis=1, keepdims=True) - 1.0
    picks = one_hot(source.astype(jnp.int32) == iota((1, slots), 1))
    push = dot(picks, found_ref[...].reshape(slots, width))
    push_ref[...] = push.astype(BF16).reshape(push_ref.shape)


def messages(batch, slot, found):
    batches, ends = slot.shape
    peers, held, width = found.shape
    return pl.pallas_call(
        functools.partial(push_kernel, batch),
        out_shape=jax.ShapeDtypeStruct((peers, held, width), BF16),
        compiler_params=params(12),
        cost_estimate=cost(1e9, 2e6),
        name="messages",
    )(slot, found)


def cos_turns(turns):
    part = turns - jnp.floor(turns + 0.5)
    square = part * part
    value = COS_TERMS[-1] * square + COS_TERMS[-2]
    for term in COS_TERMS[-3::-1]:
        value = value * square + term
    return value


def rows_at(index, found_ref):
    peers, held, width = found_ref.shape
    picks = one_hot(index.astype(jnp.int32) == iota((1, peers * held), 1))
    return dot(picks, found_ref[...].reshape(peers * held, width))


def neighbour_specs(batches):
    return [
        pl.BlockSpec((batches, 1, NBR_BLOCK), lambda g: (0, 0, g)),
        pl.BlockSpec((batches, NBR_BLOCK), lambda g: (0, g)),
    ]


def attend_kernel(
    batch,
    owner_ref,
    rank_ref,
    slot_ref,
    gap_ref,
    found_ref,
    found_end_ref,
    turn_ref,
    w_query_ref,
    w_key_value_ref,
    w_out_ref,
    *refs,
):
    out_ref = refs[-1]
    nbrs = rank_ref.shape[1]
    ends, width = nbrs // NBR, found_ref.shape[2]
    rank = rank_ref[batch : batch + 1, :]
    index = jnp.where(rank >= 0, owner_ref[batch] * found_ref.shape[1] + rank, -1)
    index, gap = columns(index, gap_ref[batch : batch + 1, :])
    rows = rows_at(index, found_ref)
    self_rows = rows_at(slot_ref[0], found_end_ref)
    encoding = cos_turns(gap * turn_ref[0:1, :] + turn_ref[1:2, :])
    keyed = (rows + encoding).astype(BF16)
    packed = dot(keyed, w_key_value_ref[...]).astype(BF16)
    query = dot(self_rows.astype(BF16), w_query_ref[...])
    head = iota((1, width), 1) // HEAD_DIM
    queries = [jnp.where(head == h, query, 0.0).astype(BF16) for h in range(HEADS)]
    score = dot_nt(jnp.concatenate(queries, axis=0), packed[:, :width]) * (1.0 / math.sqrt(HEAD_DIM))
    end = iota((HEADS * ends, 1), 0) & (ends - 1)
    place_in_end = iota((1, nbrs), 1) - NBR * end
    mine = (place_in_end >= 0) & (place_in_end < NBR) & (rank_ref[batch : batch + 1, :] >= 0)
    score = jnp.where(mine, score, -1e30)
    raised = jnp.exp(score - jnp.max(score, axis=1, keepdims=True))
    weights = (raised / jnp.sum(raised, axis=1, keepdims=True)).astype(BF16)
    mixed = dot(weights, packed[:, width:])
    attended = [
        mixed[h * ends : (h + 1) * ends, h * HEAD_DIM : (h + 1) * HEAD_DIM] for h in range(HEADS)
    ]
    attended = jnp.concatenate(attended, axis=1).astype(BF16)
    out_ref[0] = self_rows + dot(attended, w_out_ref[...])


def attend(batch, owner, rank, slot_col, gap, found, found_end, turn, weights, earlier):
    batches, nbrs = rank.shape
    peers, held, width = found.shape
    ends, end_block = nbrs // NBR, NBR_BLOCK // NBR
    specs = [
        pl.BlockSpec((batches, 1, NBR_BLOCK), lambda g: (0, 0, g)),
        pl.BlockSpec((batches, NBR_BLOCK), lambda g: (0, g)),
        pl.BlockSpec((1, end_block, 1), lambda g: (batch, g, 0)),
        pl.BlockSpec((batches, NBR_BLOCK), lambda g: (0, g)),
        whole(peers, held, width),
        whole(peers, CAP_END, width),
        whole(8, width),
        whole(width, width),
        whole(width, 2 * width),
        whole(width, width),
    ]
    aliases = {}
    if earlier:
        aliases = {len(specs): 0}
        specs += [pl.BlockSpec(memory_space=pl.ANY)]
    return pl.pallas_call(
        functools.partial(attend_kernel, batch),
        grid=(nbrs // NBR_BLOCK,),
        in_specs=specs,
        out_specs=pl.BlockSpec((1, end_block, width), lambda g: (batch, g, 0)),
        out_shape=jax.ShapeDtypeStruct((batches, ends, width), F32),
        input_output_aliases=aliases,
        compiler_params=params(28 if held <= CAP_FAST and batch == 0 else 56),
        cost_estimate=cost(2 * nbrs * width * (peers * held + 2 * width), 4 * nbrs * width),
        name="attend",
    )(owner, rank, slot_col, gap, found, found_end, turn, *weights, *earlier)


def project_kernel(memory_ref, w_input_ref, w_hidden_ref, bias_ref, out_ref):
    width = memory_ref.shape[1]
    pulled = memory_ref[...].astype(BF16)
    own = dot(pulled, w_input_ref[...]) + bias_ref[...]
    hidden = dot(pulled, w_hidden_ref[...])
    out_ref[:, : 2 * width] = own[:, : 2 * width] + hidden[:, : 2 * width]
    out_ref[:, 2 * width : 3 * width] = own[:, 2 * width :]
    out_ref[:, 3 * width :] = hidden[:, 2 * width :]


def project(memory, w_input, w_hidden, bias):
    node_dev, width = memory.shape
    block = 512
    return pl.pallas_call(
        project_kernel,
        grid=(node_dev // block,),
        in_specs=[
            pl.BlockSpec((block, width), lambda g: (g, 0)),
            whole(width, 3 * width),
            whole(width, 3 * width),
            whole(1, 3 * width),
        ],
        out_specs=pl.BlockSpec((block, 4 * width), lambda g: (g, 0)),
        out_shape=jax.ShapeDtypeStruct((node_dev, 4 * width), F32),
        compiler_params=params(48),
        cost_estimate=cost(4 * node_dev * width * 3 * width, 12e6),
        name="project_memory",
    )(memory, w_input, w_hidden, bias)


def update_kernel(
    memory_ref,
    own_ref,
    ids_ref,
    own_rows_ref,
    left_rows_ref,
    right_rows_ref,
    *refs,
):
    block, width = memory_ref.shape
    slots = own_rows_ref.shape[0]
    half = slots // 2
    outs = 2 if refs[-1].dtype == BF16 else 1
    *far_refs, w_message_ref = refs[:-outs]
    out_refs = refs[-outs:]
    far = [ref[...] for ref in far_refs]
    if len(far) == 1:
        far = [far[0][:half], far[0][half:]]
    step = pl.program_id(0)
    picks = jnp.where(ids_ref[...] == iota((block, 1), 0) + step * block, 1.0, 0.0)
    counts = jnp.sum(picks, axis=1, keepdims=True)
    picks = picks.astype(BF16)

    def summed(source, first, second):
        at = source * slots
        return dot(picks[:, at : at + half], first) + dot(picks[:, at + half : at + slots], second)

    def summed_whole(source, rows_ref):
        return summed(source, rows_ref[:half, :], rows_ref[half:, :])

    sums = (summed_whole(0, own_rows_ref) + summed(3, *far)) + (
        summed_whole(1, left_rows_ref) + summed_whole(2, right_rows_ref)
    )
    mean = sums / jnp.maximum(counts, 1.0)
    gates = dot(mean.astype(BF16), w_message_ref[...])
    memory = memory_ref[...]
    reset = jax.nn.sigmoid(own_ref[:, :width] + gates[:, :width])
    update = jax.nn.sigmoid(own_ref[:, width : 2 * width] + gates[:, width : 2 * width])
    hidden = own_ref[:, 3 * width :]
    candidate = jnp.tanh(own_ref[:, 2 * width : 3 * width] + gates[:, 2 * width :] + reset * hidden)
    new = jnp.where(counts > 0, (1.0 - update) * candidate + update * memory, memory)
    out_refs[0][...] = new
    if len(out_refs) == 2:
        out_refs[1][...] = new.astype(BF16)


def update_memory(memory, own, ids, rows, w_input, with_pulled):
    node_dev, width = memory.shape
    slots = rows[0].shape[0]
    block = UPDATE_BLOCK
    blocked = pl.BlockSpec((block, width), lambda g: (g, 0))
    types = (F32, BF16) if with_pulled else (F32,)
    return pl.pallas_call(
        update_kernel,
        grid=(node_dev // block,),
        in_specs=[
            blocked,
            pl.BlockSpec((block, 4 * width), lambda g: (g, 0)),
            whole(1, 4 * slots),
        ]
        + [whole(*part.shape) for part in rows]
        + [pl.BlockSpec((width, 3 * width), lambda g: (1, 0))],
        out_specs=tuple(blocked for _ in types),
        out_shape=tuple(jax.ShapeDtypeStruct((node_dev, width), t) for t in types),
        compiler_params=params(32 if with_pulled else 56),
        cost_estimate=cost(4e9, 1e7),
        name="memory_update",
    )(memory, own, ids, *rows, w_input)


def exchange(rows):
    return lax.all_to_all(rows, "nodes", split_axis=0, concat_axis=0, tiled=True)


def after(value, earlier):
    return lax.optimization_barrier((value, earlier))[0]


def shift(value, by):
    size = lax.axis_size("tm")
    return lax.ppermute(value, "tm", [(i, (i + by) % size) for i in range(size)])


def across_time(rows, in_hops):
    half = rows.shape[0] // 2
    left, right = shift(rows, 1), shift(rows, -1)
    if in_hops:
        return rows, left, right, shift(left[:half], 1), shift(right[half:], -1)
    return rows, left, right, shift(rows, 2)


def shards(
    memory,
    end_owner,
    end_row,
    nbr_owner,
    nbr_row,
    event_ticks,
    nbr_ticks,
    nbr_count,
    time_freq,
    time_phase,
    w_query,
    w_key_value,
    w_out,
    gru_input,
    gru_hidden,
    gru_bias,
):
    peers = lax.axis_size("nodes")
    node_dev, width = memory.shape
    batches = end_row.shape[0]
    end_owner, nbr_owner = end_owner.transpose(0, 2, 1), nbr_owner.transpose(0, 2, 1)
    ids, rank, gap, slot = place(
        node_dev, peers, end_owner, end_row, nbr_owner, nbr_row, event_ticks, nbr_ticks, nbr_count
    )
    end_range = (CAP_NBR, CAP_NBR + CAP_END)
    bias = gru_bias[None, :]
    own = project(memory, gru_input, gru_hidden, bias)
    asked, own = lax.optimization_barrier((exchange(ids), own))

    arrived_ids = asked.reshape(peers, batches, SLOTS)[:, :, CAP_NBR : CAP_NBR + CAP_END]
    arrived_ids = arrived_ids.transpose(1, 0, 2).reshape(batches, peers * CAP_END)
    load = jnp.broadcast_to(jnp.max(asked[:, 0, -1]), (1, peers * CAP_END))
    known = jnp.concatenate([arrived_ids, load])
    shared = jnp.stack([known, shift(known, 1), shift(known, -1), shift(known, 2)])
    most = jnp.max(shared[:, batches])
    all_ids = shared.transpose(1, 0, 2).reshape(batches + 1, 1, 4 * peers * CAP_END)

    turn = jnp.stack([time_freq, time_phase]) * (1.0 / (2.0 * math.pi))
    turn = jnp.concatenate([turn, jnp.zeros((6, width), F32)])
    weights = (w_query, w_key_value, w_out)
    slot_col = slot[:, :, None]

    found_end = exchange(lookup(0, (end_range,), asked, memory))
    found_end, all_ids, turn, slot_col = lax.optimization_barrier((found_end, all_ids, turn, slot_col))
    push = messages(0, slot, found_end)
    arrived = exchange(push)

    def window(cap):
        def arrivals(rows, in_hops):
            return across_time(rows.reshape(peers * CAP_END, width), in_hops)

        def embed(b, found, found_end, earlier):
            return attend(b, nbr_owner, rank, slot_col, gap, found, found_end, turn, weights, earlier)

        wanted = lookup(0, ((0, cap),), asked, memory)
        found = exchange(after(wanted, arrived))
        rows = arrivals(arrived, True)
        state, pulled_next = update_memory(memory, own, all_ids[0], rows, gru_input, True)
        wanted = lookup(1, (end_range,), asked, pulled_next)
        found_end_next = exchange(after(wanted, found))
        wanted = lookup(1, ((0, cap),), asked, pulled_next)
        own_next = project(state, gru_input, gru_hidden, bias)
        found_end_next, own_next = lax.optimization_barrier((found_end_next, own_next))
        arrived_next = exchange(messages(1, slot, found_end_next))
        found_next = exchange(after(wanted, arrived_next))
        embedded = embed(0, found, found_end, ())
        rows = arrivals(arrived_next, False)
        *rows, embedded = lax.optimization_barrier((*rows, embedded))
        (state,) = update_memory(state, own_next, all_ids[1], rows, gru_input, False)
        found_next, embedded, state = lax.optimization_barrier((found_next, embedded, state))
        embedded = embed(1, found_next, found_end_next, (embedded,))
        return embedded, state

    short = window(CAP_FAST)
    return lax.cond(most <= CAP_FAST, lambda done: done, lambda done: window(CAP_NBR), short)


def solution(mesh):
    return jax.shard_map(
        shards,
        mesh=mesh,
        in_specs=(
            P("nodes", None),
            P(None, ("nodes", "tm"), None),
            P(None, ("nodes", "tm")),
            P(None, ("nodes", "tm"), None),
            P(None, ("nodes", "tm")),
            P(None, ("nodes", "tm")),
            P(None, ("nodes", "tm")),
            P(None, ("nodes", "tm")),
            P(),
            P(),
            P(),
            P(),
            P(),
            P(),
            P(),
            P(),
        ),
        out_specs=(P(None, ("nodes", "tm"), None), P("nodes", None)),
        check_vma=False,
    )
```

```python
import functools
import math

import jax
import jax.numpy as jnp
import numpy as np
from jax import lax
from jax.experimental import pallas as pl
from jax.experimental.pallas import tpu as pltpu
from jax.sharding import PartitionSpec as P

HEADS = 4
NBR = 10
HEAD_DIM = 128
CAP_END = 16
CAP_NBR = 160
SLOTS = 256
CAP_FAST = 80
UPDATE_BLOCK = 256
NBR_BLOCK = 640
NBR_SIZES = (384, 448, NBR_BLOCK)
F32 = jnp.float32
BF16 = jnp.bfloat16
NT = (((1,), (1,)), ((), ()))
COS_TERMS = tuple(
    np.polynomial.chebyshev.Chebyshev.interpolate(
        lambda u: np.cos(2 * np.pi * np.sqrt(u)), 7, domain=[0.0, 0.25]
    )
    .convert(kind=np.polynomial.Polynomial)
    .coef.tolist()
)


def params(mib):
    return pltpu.CompilerParams(vmem_limit_bytes=mib * 1024 * 1024)


def cost(flops, size):
    return pl.CostEstimate(flops=int(flops), bytes_accessed=int(size), transcendentals=0)


def iota(shape, dim):
    return lax.broadcasted_iota(jnp.int32, shape, dim)


def whole(*shape):
    return pl.BlockSpec(shape, lambda g: (0,) * len(shape))


def one_hot(mask):
    return jnp.where(mask, 1.0, 0.0).astype(BF16)


def dot(left, right):
    return jnp.dot(left, right, preferred_element_type=F32)


def dot_nt(left, right):
    return lax.dot_general(left, right, NT, preferred_element_type=F32)


def columns(*rows):
    size = rows[0].shape[1]
    rows = [row.astype(F32) for row in rows]
    turned = jnp.concatenate(rows + [jnp.zeros((8 - len(rows), size), F32)], axis=0).T
    return [turned[:, i : i + 1] for i in range(len(rows))]


def place_kernel(
    node_dev,
    end_owner_ref,
    end_row_ref,
    nbr_owner_ref,
    nbr_row_ref,
    nbr_count_ref,
    ids_ref,
    rank_ref,
    slot_ref,
):
    batches, ends = end_row_ref.shape
    nbrs = nbr_row_ref.shape[1]
    peers = ids_ref.shape[0]
    lows = 128
    highs = node_dev // lows
    upper = one_hot(iota((ends, ends), 0) < iota((ends, ends), 1))
    group, other = iota((peers * highs, peers * highs), 0), iota((peers * highs, peers * highs), 1)
    earlier = one_hot((other < group) & (other >= group - (group & (highs - 1))))
    lane_n = iota((ends, nbrs), 1) - NBR * iota((ends, nbrs), 0)
    spread_end = one_hot((lane_n >= 0) & (lane_n < NBR))
    lane = iota((1, nbrs), 1)
    place_in_end = lane - NBR * jnp.floor((lane.astype(F32) + 0.5) * (1.0 / NBR)).astype(jnp.int32)
    counts = [nbr_count_ref[...].astype(F32), jnp.zeros((8 - batches, ends), F32)]
    count = dot(jnp.concatenate(counts, axis=0).astype(BF16), spread_end)
    peer_col = iota((peers, 1), 0)
    load = jnp.zeros((peers * highs, 1), F32)
    for b in range(batches):
        valid = place_in_end.astype(F32) < count[b : b + 1]
        nbr_owner = jnp.where(valid, nbr_owner_ref[b], -1)
        nbr_row = nbr_row_ref[b : b + 1, :]
        owned_nbr = jnp.where(nbr_owner == peer_col, 1.0, 0.0)
        owned_end = jnp.where(end_owner_ref[b] == peer_col, 1.0, 0.0)
        in_group = jnp.where(nbr_owner * highs + (nbr_row >> 7) == iota((peers * highs, 1), 0), 1.0, 0.0)
        is_low = one_hot((nbr_row & (lows - 1)) == iota((lows, 1), 0))
        asked = jnp.where(dot_nt(in_group.astype(BF16), is_low) > 0.5, 1.0, 0.0)
        totals = jnp.broadcast_to(jnp.sum(asked, axis=1, keepdims=True), asked.shape)
        offset = dot(earlier, totals.astype(BF16))
        load = jnp.maximum(load, (offset + totals)[:, 0:1])
        slot_of_row = dot(asked.astype(BF16), upper[:lows, :lows]) + offset
        nbr_rank = jnp.sum(in_group * dot(slot_of_row.astype(BF16), is_low), axis=0, keepdims=True)
        nbr_rank = jnp.where(valid, nbr_rank, -1.0)
        rank_ref[b : b + 1, :] = nbr_rank.astype(jnp.int32)
        end_rank = jnp.sum(owned_end * dot(owned_end.astype(BF16), upper), axis=0, keepdims=True)
        slot_ref[b : b + 1, :] = end_owner_ref[b] * CAP_END + end_rank.astype(jnp.int32)
        rank = jnp.concatenate([nbr_rank, end_rank + CAP_NBR], axis=1)
        at_slot = one_hot(iota((SLOTS, 1), 0).astype(F32) == rank)
        owned = jnp.concatenate([owned_nbr, owned_end], axis=1)
        row = jnp.concatenate([nbr_row, end_row_ref[b : b + 1, :]], axis=1)
        named = [(row >> 5).astype(F32), (row & 31).astype(F32), jnp.ones(row.shape, F32)]
        named = jnp.concatenate([(owned * v).astype(BF16) for v in named], axis=0)
        lists = dot_nt(named, at_slot)
        times = lists[2 * peers : 3 * peers]
        row_id = lists[0:peers] * 32.0 + lists[peers : 2 * peers]
        row_id = jnp.floor(row_id / jnp.maximum(times, 1.0) + 0.5)
        row_id = jnp.where(times > 0.5, row_id, float(node_dev))
        if b == batches - 1:
            most = jnp.max(load, axis=0, keepdims=True)
            row_id = jnp.where(iota((1, SLOTS), 1) == SLOTS - 1, most, row_id)
        ids_ref[:, 0, b * SLOTS : (b + 1) * SLOTS] = row_id.astype(jnp.int32)


def place(node_dev, peers, end_owner, end_row, nbr_owner, nbr_row, nbr_count):
    batches, ends = end_row.shape
    nbrs = nbr_row.shape[1]
    return pl.pallas_call(
        functools.partial(place_kernel, node_dev),
        out_shape=(
            jax.ShapeDtypeStruct((peers, 1, batches * SLOTS), jnp.int32),
            jax.ShapeDtypeStruct((batches, nbrs), jnp.int32),
            jax.ShapeDtypeStruct((batches, ends), jnp.int32),
        ),
        compiler_params=params(60),
        cost_estimate=cost(2e9, 1e6),
        name="request_lists",
    )(end_owner, end_row, nbr_owner, nbr_row, nbr_count)


def neighbours_kernel(
    event_ticks_ref, nbr_ticks_ref, owner_ref, rank_ref, owner_out, rank_out, gap_out, end_out, count_out
):
    batches, events = event_ticks_ref.shape
    nbrs = nbr_ticks_ref.shape[1]
    size = NBR_BLOCK
    lane = iota((events, nbrs), 1) - 2 * NBR * iota((events, nbrs), 0)
    ticks = event_ticks_ref[...]
    halves = [ticks >> 7, ticks & 127, jnp.zeros((8 - 2 * batches, events), jnp.int32)]
    halves = jnp.concatenate(halves, axis=0).astype(F32).astype(BF16)
    spread = dot(halves, one_hot((lane >= 0) & (lane < 2 * NBR)))
    event = spread[:batches] * 128.0 + spread[batches : 2 * batches]
    gap = (event - nbr_ticks_ref[...].astype(F32)).astype(jnp.int32)
    valid = jnp.where(rank_ref[...] >= 0, 1.0, 0.0)
    blocks = [(b, g * size) for b in range(batches) for g in range(nbrs // size)]
    flags = jnp.concatenate([valid[b : b + 1, at : at + size] for b, at in blocks], axis=0)
    ahead = dot(flags.astype(BF16), one_hot(iota((size, size), 0) < iota((size, size), 1)))
    ahead = jnp.where(flags > 0.5, ahead, -1.0).astype(jnp.int32)
    count_out[...] = jnp.sum(flags, axis=1, keepdims=True).astype(jnp.int32)
    end = jnp.floor((iota((1, size), 1).astype(F32) + 0.5) * (1.0 / NBR))
    for k, (b, at) in enumerate(blocks):
        lanes = slice(at, at + size)
        gaps = gap[b : b + 1, lanes]
        rows = [
            owner_ref[b, :, lanes].astype(F32),
            rank_ref[b : b + 1, lanes].astype(F32),
            (gaps >> 7).astype(F32),
            (gaps & 127).astype(F32),
            end,
            jnp.ones((1, size), F32),
            jnp.zeros((2, size), F32),
        ]
        moved = dot_nt(jnp.concatenate(rows, axis=0).astype(BF16), one_hot(iota((size, 1), 0) == ahead[k : k + 1]))
        there = moved[5:6] > 0.5
        owner_out[b : b + 1, lanes] = moved[0:1].astype(jnp.int32)
        rank_out[b : b + 1, lanes] = jnp.where(there, moved[1:2], -1.0).astype(jnp.int32)
        gap_out[b : b + 1, lanes] = moved[2:3] * 128.0 + moved[3:4]
        end_out[b : b + 1, lanes] = jnp.where(there, moved[4:5], -1.0).astype(jnp.int32)


def neighbour_lists(event_ticks, nbr_ticks, owner, rank):
    batches, nbrs = nbr_ticks.shape
    blocks = batches * (nbrs // NBR_BLOCK)
    listed = [jax.ShapeDtypeStruct((batches, nbrs), t) for t in (jnp.int32, jnp.int32, F32, jnp.int32)]
    *lists, count = pl.pallas_call(
        neighbours_kernel,
        out_shape=(*listed, jax.ShapeDtypeStruct((blocks, 1), jnp.int32)),
        compiler_params=params(32),
        cost_estimate=cost(3e9, 1e6),
        name="neighbour_lists",
    )(event_ticks, nbr_ticks, owner, rank)
    return (*lists, count.reshape(blocks))


def lookup_kernel(start, ranges, asked_ref, rows_ref, found_ref):
    node_dev = rows_ref.shape[0]
    peers, cap, width = found_ref.shape
    ids = asked_ref[:, 0, start : start + SLOTS].T
    ids = jnp.concatenate([ids[lo:hi, :] for lo, hi in ranges], axis=0)
    lane = iota((1, node_dev), 1)
    group = max(1, 512 // cap)
    group = max(g for g in (1, 2, 4, 8, 16, 32) if g <= group)
    for start in range(0, peers, group):
        picks = [
            one_hot(ids[:, p : p + 1] == lane)
            for p in range(start, start + group)
        ]
        picked = dot(jnp.concatenate(picks, axis=0), rows_ref[...])
        found_ref[start : start + group] = picked.astype(BF16).reshape(group, cap, width)


def lookup(batch, ranges, asked, pulled):
    peers = asked.shape[0]
    cap = sum(hi - lo for lo, hi in ranges)
    node_dev, width = pulled.shape
    return pl.pallas_call(
        functools.partial(lookup_kernel, batch * SLOTS, ranges),
        out_shape=jax.ShapeDtypeStruct((peers, cap, width), BF16),
        compiler_params=params(24),
        cost_estimate=cost(2 * peers * cap * node_dev * width, 2 * peers * cap * width),
        name="lookup_rows",
    )(asked, pulled)


def push_kernel(batch, slot_ref, found_ref, push_ref):
    ends = slot_ref.shape[1]
    peers, held, width = found_ref.shape
    slots = peers * held
    slot = slot_ref[batch : batch + 1, :]
    after_lane, before_lane = pltpu.roll(slot, ends - 1, 1), pltpu.roll(slot, 1, 1)
    partner = jnp.where((iota((1, ends), 1) & 1) == 0, after_lane, before_lane)
    sent = iota((slots, 1), 0) == slot
    source = jnp.sum(jnp.where(sent, partner + 1, 0).astype(F32), axis=1, keepdims=True) - 1.0
    picks = one_hot(source.astype(jnp.int32) == iota((1, slots), 1))
    push = dot(picks, found_ref[...].reshape(slots, width))
    push_ref[...] = push.astype(BF16).reshape(push_ref.shape)


def messages(batch, slot, found):
    batches, ends = slot.shape
    peers, held, width = found.shape
    return pl.pallas_call(
        functools.partial(push_kernel, batch),
        out_shape=jax.ShapeDtypeStruct((peers, held, width), BF16),
        compiler_params=params(12),
        cost_estimate=cost(1e9, 2e6),
        name="messages",
    )(slot, found)


def cos_turns(turns):
    part = turns - jnp.floor(turns + 0.5)
    square = part * part
    value = COS_TERMS[-1] * square + COS_TERMS[-2]
    for term in COS_TERMS[-3::-1]:
        value = value * square + term
    return value


def rows_at(index, found_ref):
    peers, held, width = found_ref.shape
    picks = one_hot(index.astype(jnp.int32) == iota((1, peers * held), 1))
    return dot(picks, found_ref[...].reshape(peers * held, width))


def neighbour_specs(batches):
    return [
        pl.BlockSpec((batches, 1, NBR_BLOCK), lambda g: (0, 0, g)),
        pl.BlockSpec((batches, NBR_BLOCK), lambda g: (0, g)),
    ]


def attend_kernel(
    batch,
    count_ref,
    owner_ref,
    rank_ref,
    gap_ref,
    end_ref,
    slot_ref,
    found_ref,
    found_end_ref,
    turn_ref,
    w_query_ref,
    w_key_value_ref,
    w_out_ref,
    *refs,
):
    out_ref = refs[-1]
    ends, width = NBR_BLOCK // NBR, found_ref.shape[2]

    def with_neighbours(size):
        rank = rank_ref[batch : batch + 1, :size]
        index = jnp.where(rank >= 0, owner_ref[batch : batch + 1, :size] * found_ref.shape[1] + rank, -1)
        index, gap = columns(index, gap_ref[batch : batch + 1, :size])
        rows = rows_at(index, found_ref)
        self_rows = rows_at(slot_ref[0], found_end_ref)
        encoding = cos_turns(gap * turn_ref[0:1, :] + turn_ref[1:2, :])
        keyed = (rows + encoding).astype(BF16)
        packed = dot(keyed, w_key_value_ref[...]).astype(BF16)
        query = dot(self_rows.astype(BF16), w_query_ref[...])
        head = iota((1, width), 1) // HEAD_DIM
        queries = [jnp.where(head == h, query, 0.0).astype(BF16) for h in range(HEADS)]
        score = dot_nt(jnp.concatenate(queries, axis=0), packed[:, :width]) * (1.0 / math.sqrt(HEAD_DIM))
        mine = end_ref[batch : batch + 1, :size] == (iota((HEADS * ends, 1), 0) & (ends - 1))
        score = jnp.where(mine, score, -1e30)
        raised = jnp.exp(score - jnp.max(score, axis=1, keepdims=True))
        weights = (raised / jnp.sum(raised, axis=1, keepdims=True)).astype(BF16)
        mixed = dot(weights, packed[:, width:])
        attended = [
            mixed[h * ends : (h + 1) * ends, h * HEAD_DIM : (h + 1) * HEAD_DIM] for h in range(HEADS)
        ]
        attended = jnp.concatenate(attended, axis=1).astype(BF16)
        out_ref[0] = self_rows + dot(attended, w_out_ref[...])

    count = count_ref[batch * pl.num_programs(0) + pl.program_id(0)]
    least = -1
    for size in NBR_SIZES:

        @pl.when((count > least) & (count <= size))
        def _(size=size):
            with_neighbours(size)

        least = size


def attend(batch, lists, slot_col, found, found_end, turn, weights, earlier):
    owner, rank, gap, end, count = lists
    batches, nbrs = rank.shape
    peers, held, width = found.shape
    ends, end_block = nbrs // NBR, NBR_BLOCK // NBR
    specs = (
        [pl.BlockSpec(memory_space=pltpu.SMEM)]
        + [pl.BlockSpec((batches, NBR_BLOCK), lambda g: (0, g)) for _ in range(4)]
        + [
            pl.BlockSpec((1, end_block, 1), lambda g: (batch, g, 0)),
            whole(peers, held, width),
            whole(peers, CAP_END, width),
            whole(8, width),
            whole(width, width),
            whole(width, 2 * width),
            whole(width, width),
        ]
    )
    aliases = {}
    if earlier:
        aliases = {len(specs): 0}
        specs += [pl.BlockSpec(memory_space=pl.ANY)]
    return pl.pallas_call(
        functools.partial(attend_kernel, batch),
        grid=(nbrs // NBR_BLOCK,),
        in_specs=specs,
        out_specs=pl.BlockSpec((1, end_block, width), lambda g: (batch, g, 0)),
        out_shape=jax.ShapeDtypeStruct((batches, ends, width), F32),
        input_output_aliases=aliases,
        compiler_params=params(28 if held <= CAP_FAST and batch == 0 else 56),
        cost_estimate=cost(2 * nbrs * width * (peers * held + 2 * width), 4 * nbrs * width),
        name="attend",
    )(count, owner, rank, gap, end, slot_col, found, found_end, turn, *weights, *earlier)


def project_kernel(memory_ref, w_input_ref, w_hidden_ref, bias_ref, out_ref, pulled_ref):
    width = memory_ref.shape[1]
    pulled = memory_ref[...].astype(BF16)
    own = dot(pulled, w_input_ref[...]) + bias_ref[...]
    hidden = dot(pulled, w_hidden_ref[...])
    out_ref[:, : 2 * width] = own[:, : 2 * width] + hidden[:, : 2 * width]
    out_ref[:, 2 * width : 3 * width] = own[:, 2 * width :]
    out_ref[:, 3 * width :] = hidden[:, 2 * width :]
    pulled_ref[...] = pulled


def project(memory, w_input, w_hidden, bias):
    node_dev, width = memory.shape
    block = 512
    return pl.pallas_call(
        project_kernel,
        grid=(node_dev // block,),
        in_specs=[
            pl.BlockSpec((block, width), lambda g: (g, 0)),
            whole(width, 3 * width),
            whole(width, 3 * width),
            whole(1, 3 * width),
        ],
        out_specs=(
            pl.BlockSpec((block, 4 * width), lambda g: (g, 0)),
            pl.BlockSpec((block, width), lambda g: (g, 0)),
        ),
        out_shape=(
            jax.ShapeDtypeStruct((node_dev, 4 * width), F32),
            jax.ShapeDtypeStruct((node_dev, width), BF16),
        ),
        compiler_params=params(58),
        cost_estimate=cost(4 * node_dev * width * 3 * width, 12e6),
        name="project_memory",
    )(memory, w_input, w_hidden, bias)


def update_kernel(
    memory_ref,
    own_ref,
    ids_ref,
    own_rows_ref,
    *refs,
):
    block, width = memory_ref.shape
    slots = own_rows_ref.shape[0]
    half = slots // 2
    outs = 2 if refs[-1].dtype == BF16 else 1
    *parts, w_message_ref = refs[:-outs]
    out_refs = refs[-outs:]
    rows = [own_rows_ref[:half, :], own_rows_ref[half:, :]]
    for part in parts:
        rows += [part[...]] if part.shape[0] == half else [part[:half, :], part[half:, :]]
    step = pl.program_id(0)
    picks = jnp.where(ids_ref[...] == iota((block, 1), 0) + step * block, 1.0, 0.0)
    counts = jnp.sum(picks, axis=1, keepdims=True)
    picks = picks.astype(BF16)

    def summed(source):
        at = source * slots
        first, second = picks[:, at : at + half], picks[:, at + half : at + slots]
        return dot(first, rows[2 * source]) + dot(second, rows[2 * source + 1])

    sums = (summed(0) + summed(3)) + (summed(1) + summed(2))
    mean = sums / jnp.maximum(counts, 1.0)
    gates = dot(mean.astype(BF16), w_message_ref[...])
    memory = memory_ref[...]
    reset = jax.nn.sigmoid(own_ref[:, :width] + gates[:, :width])
    update = jax.nn.sigmoid(own_ref[:, width : 2 * width] + gates[:, width : 2 * width])
    hidden = own_ref[:, 3 * width :]
    candidate = jnp.tanh(own_ref[:, 2 * width : 3 * width] + gates[:, 2 * width :] + reset * hidden)
    new = jnp.where(counts > 0, (1.0 - update) * candidate + update * memory, memory)
    out_refs[0][...] = new
    if len(out_refs) == 2:
        out_refs[1][...] = new.astype(BF16)


def update_memory(memory, own, ids, rows, w_input, with_pulled):
    node_dev, width = memory.shape
    slots = rows[0].shape[0]
    block = UPDATE_BLOCK
    blocked = pl.BlockSpec((block, width), lambda g: (g, 0))
    types = (F32, BF16) if with_pulled else (F32,)
    return pl.pallas_call(
        update_kernel,
        grid=(node_dev // block,),
        in_specs=[
            blocked,
            pl.BlockSpec((block, 4 * width), lambda g: (g, 0)),
            whole(1, 4 * slots),
        ]
        + [whole(*part.shape) for part in rows]
        + [pl.BlockSpec((width, 3 * width), lambda g: (1, 0))],
        out_specs=tuple(blocked for _ in types),
        out_shape=tuple(jax.ShapeDtypeStruct((node_dev, width), t) for t in types),
        compiler_params=params(32 if with_pulled else 56),
        cost_estimate=cost(4e9, 1e7),
        name="memory_update",
    )(memory, own, ids, *rows, w_input)


def exchange(rows):
    return lax.all_to_all(rows, "nodes", split_axis=0, concat_axis=0, tiled=True)


def after(value, earlier):
    return lax.optimization_barrier((value, earlier))[0]


def shift(value, by):
    size = lax.axis_size("tm")
    return lax.ppermute(value, "tm", [(i, (i + by) % size) for i in range(size)])


def across_time(rows, in_hops):
    half = rows.shape[0] // 2
    if in_hops:
        first, second = rows[:half], rows[half:]
        left_first, right_second = shift(first, 1), shift(second, -1)
        left_second, right_first = shift(second, 1), shift(first, -1)
        far_first, far_second = shift(left_first, 1), shift(right_second, -1)
        pairs = (left_first, left_second), (right_first, right_second), (far_first, far_second)
    else:
        pairs = (shift(rows, 1),), (shift(rows, -1),), (shift(rows, 2),)
    return (rows, *(part for pair in pairs for part in pair))


def shards(
    memory,
    end_owner,
    end_row,
    nbr_owner,
    nbr_row,
    event_ticks,
    nbr_ticks,
    nbr_count,
    time_freq,
    time_phase,
    w_query,
    w_key_value,
    w_out,
    gru_input,
    gru_hidden,
    gru_bias,
):
    peers = lax.axis_size("nodes")
    node_dev, width = memory.shape
    batches = end_row.shape[0]
    end_owner, nbr_owner = end_owner.transpose(0, 2, 1), nbr_owner.transpose(0, 2, 1)
    ids, rank, slot = place(node_dev, peers, end_owner, end_row, nbr_owner, nbr_row, nbr_count)
    lists = neighbour_lists(event_ticks, nbr_ticks, nbr_owner, rank)
    end_range = (CAP_NBR, CAP_NBR + CAP_END)
    bias = gru_bias[None, :]
    own, pulled = project(memory, gru_input, gru_hidden, bias)
    asked, own, pulled = lax.optimization_barrier((exchange(ids), own, pulled))

    turn = jnp.stack([time_freq, time_phase]) * (1.0 / (2.0 * math.pi))
    turn = jnp.concatenate([turn, jnp.zeros((6, width), F32)])
    weights = (w_query, w_key_value, w_out)
    slot_col = slot[:, :, None]

    found_end = exchange(lookup(0, (end_range,), asked, pulled))
    wanted_first = lookup(0, ((0, CAP_FAST),), asked, pulled)
    found_end, wanted_first, turn, slot_col, *lists = lax.optimization_barrier(
        (found_end, wanted_first, turn, slot_col, *lists)
    )
    arrived_ids = asked.reshape(peers, batches, SLOTS)[:, :, CAP_NBR : CAP_NBR + CAP_END]
    arrived_ids = arrived_ids.transpose(1, 0, 2).reshape(batches, peers * CAP_END)
    load = jnp.broadcast_to(jnp.max(asked[:, 0, -1]), (1, peers * CAP_END))
    known = after(jnp.concatenate([arrived_ids, load]), found_end)
    shared = jnp.stack([known, shift(known, 1), shift(known, -1), shift(known, 2)])
    most = jnp.max(shared[:, batches])
    all_ids = shared.transpose(1, 0, 2).reshape(batches + 1, 1, 4 * peers * CAP_END)

    push = messages(0, slot, found_end)
    arrived, all_ids, most = lax.optimization_barrier((exchange(push), all_ids, most))

    def window(cap, wanted):
        def arrivals(rows, in_hops):
            return across_time(rows.reshape(peers * CAP_END, width), in_hops)

        def embed(b, found, found_end, earlier):
            return attend(b, lists, slot_col, found, found_end, turn, weights, earlier)

        found = exchange(after(wanted, arrived))
        rows = arrivals(arrived, True)
        state, pulled_next = update_memory(memory, own, all_ids[0], rows, gru_input, True)
        wanted = lookup(1, (end_range,), asked, pulled_next)
        found_end_next = exchange(after(wanted, found))
        wanted = lookup(1, ((0, cap),), asked, pulled_next)
        own_next, _ = project(state, gru_input, gru_hidden, bias)
        found_end_next, own_next = lax.optimization_barrier((found_end_next, own_next))
        arrived_next = exchange(messages(1, slot, found_end_next))
        found_next = exchange(after(wanted, arrived_next))
        embedded = embed(0, found, found_end, ())
        rows = arrivals(arrived_next, False)
        *rows, embedded = lax.optimization_barrier((*rows, embedded))
        (state,) = update_memory(state, own_next, all_ids[1], rows, gru_input, False)
        found_next, embedded, state = lax.optimization_barrier((found_next, embedded, state))
        embedded = embed(1, found_next, found_end_next, (embedded,))
        return embedded, state

    def long_window():
        return window(CAP_NBR, lookup(0, ((0, CAP_NBR),), asked, pulled))

    short = window(CAP_FAST, wanted_first)
    return lax.cond(most <= CAP_FAST, lambda done: done, lambda done: long_window(), short)


def solution(mesh):
    return jax.shard_map(
        shards,
        mesh=mesh,
        in_specs=(
            P("nodes", None),
            P(None, ("nodes", "tm"), None),
            P(None, ("nodes", "tm")),
            P(None, ("nodes", "tm"), None),
            P(None, ("nodes", "tm")),
            P(None, ("nodes", "tm")),
            P(None, ("nodes", "tm")),
            P(None, ("nodes", "tm")),
            P(),
            P(),
            P(),
            P(),
            P(),
            P(),
            P(),
            P(),
        ),
        out_specs=(P(None, ("nodes", "tm"), None), P("nodes", None)),
        check_vma=False,
    )
```
